32 devices in a mesh: dom: 16 (over z, x, core), frame: 2 (over y).
Axes of the slice: x: 2, y: 2, z: 4, core: 2. Of those that a mesh axis runs over, the one named last changes fastest.
Arguments:
- features: bfloat16 [2048, 512], P('dom'), may hold values from -6 to 6
- positions: bfloat16 [3, 2048], P(None, 'dom'), may hold values from 0 to 4
- neighbours: int32 [2048, 128], P('dom'), may hold values from 0 to 255, as said below
- counts: int32 [2048], P('dom'), may hold values from 1 to 128, as said below
- send_rows: int32 [16, 2, 64], P('dom'), may hold values from 0 to 127
- frames: float32 [2, 3, 3], P('frame')
- w_edge: float32 [9, 512], replicated, may hold values from -2 to 2
- b_edge: float32 [512], replicated, may hold values from -4 to 4
- w_message: bfloat16 [512, 512], replicated, may hold values from -0.25 to 0.25
- w_update: bfloat16 [512, 512], replicated, may hold values from -0.25 to 0.25
- w_readout: bfloat16 [512, 512], replicated, may hold values from -0.25 to 0.25
- w_heads: bfloat16 [512, 4], replicated, may hold values from -0.25 to 0.25
Outputs:
- predictions: float32 [4, 2048], P(None, 'dom')
The draws below stay inside these ranges and needn't reach their ends.
Inputs may be any that keep to these rules, and one draw needn't show every extreme that they name: `counts`: each domain has its own largest count, one of 32, 64, 96 or 128, reached by one of its atoms; some domain reaches 128. `neighbours`: order a domain's table as the 64 rows from the domain below, its own 128 atoms, then the 64 rows from the domain above; every slot of an atom in aligned block b of 16 atoms of its domain names a row at positions (b * 128) // max(7, 1) to that plus 128 - 1 of this order.
All inputs are finite; a program needn't handle non-finite values.
Results may differ from the reference program's by a relative error of at most 0.0049.
Values may be sent and summed in bfloat16 or wider, within the bound.
A program may use at most 64 MiB of HBM per device.

```python
import math
import jax
import jax.numpy as jnp
from jax import lax

W = 512
RBF = 6
NEIGH = 128
WINDOW = 128
ATOMS_DEV = 128
CAP = 64
ATOMS = 2048
N_DOM = 16
N_FRAME = 2


def draw_neighbours(key, part):
    table_rows = ATOMS_DEV + 2 * CAP
    block_total = ATOMS_DEV // 16
    span_rows = table_rows - WINDOW
    denom = max(block_total - 1, 1)
    starts = jnp.arange(block_total, dtype=jnp.int32) * span_rows // denom
    offsets = jax.random.randint(jax.random.fold_in(key, 31), (N_DOM, block_total, 16, NEIGH), 0, WINDOW)
    placed = starts[None, :, None, None] + offsets
    placed = placed.at[:, block_total - 1, 0, 0].set(table_rows - 1)
    zero_block = min(CAP * (block_total - 1) // max(span_rows, 1), block_total - 1)
    placed = placed.at[:, zero_block, 0, 1].set(CAP)
    values = jnp.where(placed < CAP, ATOMS_DEV + placed, jnp.where(placed < CAP + ATOMS_DEV, placed - CAP, placed))
    return values.reshape(N_DOM * ATOMS_DEV, NEIGH).astype(jnp.int32)


def draw_counts(key, part):
    key_order = jax.random.fold_in(key, 11)
    key_count = jax.random.fold_in(key, 12)
    key_peak = jax.random.fold_in(key, 13)
    order = jax.random.permutation(key_order, N_DOM)
    density = 1 + order % 4
    density_top = NEIGH * density // 4
    raw_draw = jax.random.randint(key_count, (N_DOM, ATOMS_DEV), 0, 1 << 20)
    drawn = raw_draw % density_top[:, None] + 1
    peak_spot = jax.random.randint(key_peak, (N_DOM, 1), 0, ATOMS_DEV)
    peak_mask = jnp.arange(ATOMS_DEV)[None, :] == peak_spot
    return jnp.where(peak_mask, density_top[:, None], drawn).reshape(-1).astype(jnp.int32)


def draw_frames(key, part):
    key_angle = jax.random.fold_in(key, 21)
    angles = jax.random.uniform(key_angle, (3,), jnp.float32, -math.pi, math.pi)
    cosines = jnp.cos(angles)
    sines = jnp.sin(angles)
    basis = jnp.stack([cosines[1] * cosines[0], cosines[0] * sines[1] * sines[2] - sines[0] * cosines[2], cosines[0] * sines[1] * cosines[2] + sines[0] * sines[2], cosines[1] * sines[0], sines[0] * sines[1] * sines[2] + cosines[0] * cosines[2], sines[0] * sines[1] * cosines[2] - cosines[0] * sines[2], -sines[1], cosines[1] * sines[2], cosines[1] * cosines[2]]).reshape(3, 3)
    flips = jnp.arange(N_FRAME, dtype=jnp.int32)[:, None] >> jnp.arange(3, dtype=jnp.int32)[None, :] & 1
    signs = 1.0 - 2.0 * flips.astype(jnp.float32)
    return (signs[:, :, None] * basis[None, :, :]).astype(jnp.float32)


def set_ends(entries, own_key, low, top_value):
    spot = [jax.random.randint(jax.random.fold_in(own_key, axis), (), 0, length) for axis, length in enumerate(entries.shape)]
    main_axis = entries.shape.index(max(entries.shape))
    beside = spot[:main_axis] + [(spot[main_axis] + 1) % entries.shape[main_axis]] + spot[main_axis + 1:]
    return entries.at[tuple(spot)].set(low).at[tuple(beside)].set(top_value)


def levels(rng, extent, cuts, low, largest):
    loudness = 1.0
    for position, shards_of in cuts:
        heights = jax.random.uniform(jax.random.fold_in(jax.random.fold_in(rng, 6), position), (shards_of,), jnp.float32, low / len(cuts), largest / len(cuts))
        loudness = loudness * jnp.repeat(jnp.exp(heights), extent[position] // shards_of).reshape((-1,) + (1,) * (len(extent) - 1 - position))
    return loudness


def gaussian(rng, shape, scale, most, shards=(), held_as=jnp.bfloat16):
    values = jax.random.normal(rng, shape, jnp.float32) * scale
    if len(shards) > 0:
        values = levels(rng, shape, shards, -0.22, 0.18) * values
    return jnp.clip(values, min=-most, max=most).astype(held_as)


def setup_inputs(seed: int = 0) -> dict:
    streams_of = jax.random.split(jax.random.key(seed), 13)
    features = gaussian(streams_of[0], (ATOMS, W), 1.0, 6.0, ((0, 16),))
    positions = jnp.clip(4.0 * jax.random.uniform(streams_of[1], (3, ATOMS), jnp.float32) ** levels(streams_of[1], (3, ATOMS), ((1, 16),), -0.2, 0.2), 0.0, 4.0).astype(jnp.bfloat16)
    neighbours = draw_neighbours(jax.random.fold_in(streams_of[12], 71), 0)
    counts = draw_counts(jax.random.fold_in(streams_of[12], 71), 0)
    send_rows = set_ends(jax.random.randint(streams_of[4], (N_DOM, 2, CAP), 0, ATOMS_DEV), jax.random.fold_in(streams_of[4], 1), 0, ATOMS_DEV - 1).astype(jnp.int32)
    frames = draw_frames(jax.random.fold_in(streams_of[12], 71), 0)
    w_edge = gaussian(streams_of[6], (RBF + 3, W), (RBF + 3) ** -0.5, 2.0, (), jnp.float32)
    b_edge = gaussian(streams_of[7], (W,), 1.0, 4.0, (), jnp.float32)
    w_message = gaussian(streams_of[8], (W, W), W ** -0.5, 0.25)
    w_update = gaussian(streams_of[9], (W, W), W ** -0.5, 0.25)
    w_readout = gaussian(streams_of[10], (W, W), W ** -0.5, 0.25)
    w_heads = gaussian(streams_of[11], (W, 4), W ** -0.5, 0.25)
    return dict(features=features, positions=positions, neighbours=neighbours, counts=counts, send_rows=send_rows, frames=frames, w_edge=w_edge, b_edge=b_edge, w_message=w_message, w_update=w_update, w_readout=w_readout, w_heads=w_heads)


message_scale = 0.0884
radial_step = 1.25

def edge_messages(rows_feat, rows_pos, centre_pos, live_mask, rotation, w_edge, b_edge):
    relative = rows_pos - centre_pos[:, None, :]
    frame_vec = jnp.einsum('bkc,ac->bka', relative, rotation, precision=lax.Precision.HIGHEST)
    distance = jnp.sqrt(lax.optimization_barrier(jnp.sum(relative * relative, axis=-1)) + 0.25)
    centres = jnp.arange(w_edge.shape[0] - 3, dtype=jnp.float32) * radial_step
    radial = jnp.exp(-(distance[..., None] - centres) ** 2)
    edge_in = jnp.concatenate([radial, frame_vec], axis=-1)
    preact = jnp.einsum('bki,iw->bkw', edge_in, w_edge, precision=lax.Precision.HIGHEST) + b_edge
    edge_gate = jax.nn.silu(preact) * live_mask[..., None]
    return lax.optimization_barrier(jnp.sum(edge_gate * rows_feat.astype(jnp.float32), axis=1)) * message_scale

def reference(features, positions, neighbours, counts, send_rows, frames, w_edge, b_edge, w_message, w_update, w_readout, w_heads):
    domain_ids = jnp.arange(N_DOM, dtype=jnp.int32)
    lower_src = ((domain_ids - 1) % N_DOM).astype(jnp.int32)
    upper_src = ((domain_ids + 1) % N_DOM).astype(jnp.int32)
    ghost_lower = lower_src[:, None] * ATOMS_DEV + send_rows[lower_src, 1, :].astype(jnp.int32)
    ghost_upper = upper_src[:, None] * ATOMS_DEV + send_rows[upper_src, 0, :].astype(jnp.int32)
    ghost_global = jnp.concatenate([ghost_lower, ghost_upper], axis=1).astype(jnp.int32)
    own_global = domain_ids[:, None] * ATOMS_DEV + jnp.arange(ATOMS_DEV, dtype=jnp.int32)[None, :]
    lookup = jnp.concatenate([own_global, ghost_global], axis=1)
    edge_global = jnp.take_along_axis(lookup, neighbours.reshape(N_DOM, ATOMS_DEV * NEIGH).astype(jnp.int32), axis=1).reshape(ATOMS, NEIGH)
    coords = positions.astype(jnp.float32).T
    slot_index = jnp.arange(NEIGH, dtype=jnp.int32)[None, :]

    def one_frame(rotation):

        def one_block(block_in):
            block_idx, block_count, block_centre = block_in
            live_mask = (slot_index < block_count[:, None]).astype(jnp.float32)
            return edge_messages(features[block_idx], coords[block_idx], block_centre, live_mask, rotation, w_edge, b_edge)
        message = lax.map(one_block, (edge_global.reshape(-1, 16, NEIGH), counts.reshape(-1, 16), coords.reshape(-1, 16, 3)))
        message = message.reshape(ATOMS, W).astype(jnp.bfloat16)
        hidden = jax.nn.silu(jnp.dot(message, w_message, preferred_element_type=jnp.float32)).astype(jnp.bfloat16)
        updated = (features.astype(jnp.float32) + jnp.dot(hidden, w_update, preferred_element_type=jnp.float32)).astype(jnp.bfloat16)
        readout = jax.nn.silu(jnp.dot(updated, w_readout, preferred_element_type=jnp.float32)).astype(jnp.bfloat16)
        heads = jnp.dot(readout, w_heads, preferred_element_type=jnp.float32)
        force_can = jnp.einsum('na,ac->cn', heads[:, :3], rotation, precision=lax.Precision.HIGHEST)
        return jnp.concatenate([force_can, heads[:, 3][None, :]], axis=0)
    frame_terms = lax.map(one_frame, frames)
    return lax.optimization_barrier(jnp.sum(frame_terms, axis=0)) / N_FRAME
```

```python
import functools

import jax
import jax.numpy as jnp
from jax import lax
from jax.experimental import pallas as pl
from jax.experimental.pallas import tpu as pltpu
from jax.sharding import PartitionSpec as P

F32 = jnp.float32
BF16 = jnp.bfloat16
MESH = pl.DeviceIdType.MESH
WINDOW = 128
message_scale = 0.0884
radial_step = 1.25
block_atoms = 16
UNROLL = 2


def iota(shape, dim):
    return lax.broadcasted_iota(jnp.int32, shape, dim)


def dot(a, b):
    return jnp.dot(a, b, preferred_element_type=F32)


def split(value):
    high = value.astype(BF16).astype(F32)
    return high, value - high


def silu(x):
    half = 0.5 * x
    return half + half * jnp.tanh(half)


def up16(n):
    return (n + 15) // 16 * 16


def chunk_sizes(F, atoms, cap):
    blocks = atoms // block_atoms
    per = blocks // F
    span = atoms + 2 * cap - WINDOW
    own, ghost = [0] * per, [0] * per
    for f in range(F):
        for b in range(f * per, (f + 1) * per):
            start = b * span // max(blocks - 1, 1)
            low, high = max(start - cap, 0), min(start + WINDOW - cap, atoms)
            below, above = max(cap - start, 0), max(start + WINDOW - cap - atoms, 0)
            if f < F // 2:
                assert above == 0
                l, need, gh = b - f * per, high, below
            else:
                assert below == 0
                l, need, gh = (f + 1) * per - 1 - b, atoms - low, above
            own[l] = max(own[l], up16(need))
            ghost[l] = max(ghost[l], up16(gh))
    return own, ghost


def kernel(
    F, D, atoms, cap, width,
    feat, pos, nbr, cnt, send, frames, w_edge, b_edge, w_msg_h, w_upd_h, w_read_h, w_heads,
    out,
    table, cols, nbr_s, add_s, own_u, send_buf, ghost_buf, lhs, fr_stage, fr_s, base_s, wst,
    msg_s, z_s, fin_stage, fin_s, w_msg, w_upd, w_read,
    w_sem, halo_send, halo_recv, fr_send, fr_recv, fin_send, fin_recv,
):
    f = lax.axis_index("frame")
    d = lax.axis_index("dom")
    side = f // (F // 2)
    blocks = atoms // block_atoms
    per = blocks // F
    nat = per * block_atoms
    own_n, ghost_n = chunk_sizes(F, atoms, cap)
    region = atoms + cap
    first = f * nat

    barrier = pltpu.get_barrier_semaphore()
    peers = [lax.rem(f + k, F) for k in range(1, F)]
    up, down = lax.rem(d + 1, D), lax.rem(d + D - 1, D)
    for peer in peers:
        pl.semaphore_signal(barrier, inc=1, device_id={"frame": peer}, device_id_type=MESH)
    for near in (up, down):
        pl.semaphore_signal(barrier, inc=1, device_id={"dom": near}, device_id_type=MESH)
    weight_copies = [
        pltpu.make_async_copy(src, dst, w_sem.at[n])
        for n, (src, dst) in enumerate(((w_msg_h, w_msg), (w_upd_h, w_upd), (w_read_h, w_read)))
    ]
    for copy in weight_copies:
        copy.start()

    lane = iota((128, 128), 1)
    row = iota((128, 128), 0)

    table[...] = jnp.zeros_like(table)
    table[0:3, :] = pos[...].astype(F32)
    table[3:4, :] = cnt[...].astype(F32)
    by_atom = table[...].T
    sq = jnp.sum(jnp.where(lane < 3, by_atom * by_atom, 0.0), axis=1, keepdims=True)
    sq_hi, rest = split(sq)
    sq_mid, sq_lo = split(rest)
    u = jnp.where(lane < 3, by_atom, 0.0)
    u = jnp.where(lane == 3, sq_hi, u)
    u = jnp.where(lane == 4, sq_mid, u)
    u = jnp.where(lane == 5, sq_lo, u)
    u = jnp.where((lane >= 6) & (lane < 9), 1.0, u)
    own_u[...] = u.astype(BF16)

    fr_stage[...] = jnp.zeros_like(fr_stage)
    for a in range(3):
        fr_stage[a : a + 1, 0:3] = frames[a]
    fr_s[f] = fr_stage[...]
    chosen = jnp.where(side == 0, send[1:2, :], send[0:1, :])
    pick = (iota((atoms, cap), 0) == chosen).astype(F32).T.astype(BF16)
    send_buf[:, 0:width] = dot(pick, feat[...]).astype(BF16)
    send_buf[:, width : width + 128] = dot(pick, own_u[...]).astype(BF16)

    pl.semaphore_wait(barrier, F + 1)
    target = jnp.where(side == 0, up, down)
    halo = pltpu.make_async_remote_copy(
        src_ref=send_buf, dst_ref=ghost_buf, send_sem=halo_send, recv_sem=halo_recv,
        device_id={"dom": target}, device_id_type=MESH,
    )
    fr_copies = [
        pltpu.make_async_remote_copy(
            src_ref=fr_stage, dst_ref=fr_s.at[f], send_sem=fr_send.at[k], recv_sem=fr_recv.at[k],
            device_id={"frame": peer}, device_id_type=MESH,
        )
        for k, peer in enumerate(peers)
    ]
    for copy in fr_copies:
        copy.start()
    halo.start()

    live = iota((atoms, nbr.shape[1]), 1).astype(F32) < by_atom[:, 3:4]
    nbr_s[...] = jnp.where(live, nbr[...].astype(F32), -1.0)

    radial = lane % 8
    spot = (lane // 8) * 2 + radial - 6
    special = radial >= 6
    place = special & (spot < 6) & (row < 3) & (row == spot % 3)
    place_neg = special & (spot >= 6) & (spot < 12) & (row < 3) & (row == spot % 3)
    place_one = special & (spot >= 12) & (spot < 14) & (row == 6)
    place_add = jnp.where(place_one, 1.0, jnp.where(place_neg, -1.0, 0.0)).astype(BF16)
    add_s[...] = dot(own_u[...], place_add)
    place = jnp.where(place, 1.0, 0.0).astype(BF16)
    centres = radial[0:1, :].astype(F32) * radial_step

    def block_rows(l):
        return (l * (1 - side) + (per - 1 - l) * side) * block_atoms

    def own_base(l):
        return pl.multiple_of(side * (atoms - own_n[l]), 16)

    def ghost_base(l):
        return pl.multiple_of((1 - side) * (cap - ghost_n[l]), 16)

    def geometry(l):
        start = first + block_rows(l)
        expand = jnp.where(row == start + lane // 8, 1.0, 0.0).astype(BF16)
        centre = dot(table[0:16, :].astype(BF16), expand)
        sub = iota((16, 128), 0)
        sqi = jnp.sum(jnp.where(sub < 3, centre * centre, 0.0), axis=0, keepdims=True) + 0.25
        hi, tail = split(sqi)
        mid, lo = split(tail)
        g = jnp.where((row >= 3) & (row < 6), 1.0, 0.0)
        for c in range(3):
            g = jnp.where(row == c, -2.0 * centre[c : c + 1, :], g)
        for c, part in enumerate((hi, mid, lo)):
            g = jnp.where(row == 6 + c, part, g)
        return g.astype(BF16)

    def fill(l, g, rows_u, offset):
        n = rows_u.shape[0]
        d2 = dot(rows_u, g)
        placed = dot(rows_u, place)
        dist = jnp.sqrt(jnp.maximum(d2, 0.25))
        gap = dist - centres
        value = jnp.exp(-(gap * gap))
        spec = special[0:n, :]
        lhs[l * region + offset : l * region + offset + n, 0:128] = jnp.where(spec, 0.0, value).astype(BF16)
        lhs[l * region + offset : l * region + offset + n, 128:256] = jnp.where(spec, placed, value).astype(BF16)

    gs = []
    for l in range(per):
        g = geometry(l)
        gs.append(g)
        fill(l, g, own_u[pl.ds(own_base(l), own_n[l]), :], 0)

    r = iota((256, 32), 0)
    c = iota((256, 32), 1)
    rb = r % 8
    rs = (r % 128) // 8 * 2 + rb - 6
    second = r // 128
    want = jnp.where(rb < 6, second * 6 + rb, -1)
    sp = (rb >= 6) & (second == 1)
    want = jnp.where(sp & (rs < 3), 12 + rs, want)
    want = jnp.where(sp & (rs >= 3) & (rs < 6), 12 + rs, want)
    want = jnp.where(sp & (rs >= 6) & (rs < 12), 6 + rs, want)
    want = jnp.where(sp & (rs >= 12) & (rs < 14), 6 + rs, want)
    sel = jnp.where(want == c, 1.0, 0.0).astype(BF16)
    base_s[...] = jnp.zeros_like(base_s)
    hi, lo = split(0.5 * w_edge[0:6, :])
    base_s[0:6, :] = hi
    base_s[6:12, :] = lo
    hi, lo = split(0.5 * b_edge[...])
    base_s[18:19, :] = hi
    base_s[19:20, :] = lo
    for copy in fr_copies:
        copy.wait()
    for fr in range(F):
        for cc in range(3):
            acc = fr_s[fr, 0:1, cc : cc + 1] * w_edge[6:7, :]
            acc = acc + fr_s[fr, 1:2, cc : cc + 1] * w_edge[7:8, :]
            acc = acc + fr_s[fr, 2:3, cc : cc + 1] * w_edge[8:9, :]
            hi, lo = split(0.5 * acc)
            base_s[12 + cc : 13 + cc, :] = hi
            base_s[15 + cc : 16 + cc, :] = lo
        wst[:, fr * width : (fr + 1) * width] = dot(sel, base_s[...].astype(BF16)).astype(BF16)

    lane1 = iota((1, 128), 1)
    group = lane1 // 8
    special1 = lane1 % 8 >= 6

    def atom(l, i, n, offset, first_id, load_feat, add):
        local = block_rows(l) + i
        ids = (first_id + iota((n, 128), 0)).astype(F32)
        named = nbr_s[pl.ds(first + local, 1), :]
        mult = jnp.sum(jnp.where(ids == named, 1.0, 0.0), axis=1, keepdims=True)
        weighted = load_feat() * mult.astype(BF16)
        mask = jnp.where((group == i) & (~special1), 1.0, 0.0)
        extra = add_s[pl.ds(first + local, 1), :]
        left1 = lhs[l * region + offset : l * region + offset + n, 0:128] * mask.astype(BF16)
        left2 = lhs[l * region + offset : l * region + offset + n, 128:256]
        left2 = left2 * jnp.where(special1, 1.0, mask).astype(BF16) + extra.astype(BF16)
        left = jnp.concatenate([left1, left2], axis=1)
        for fr in range(F):
            h = dot(left, wst[:, fr * width : (fr + 1) * width]).astype(BF16)
            terms = (h + h * jnp.tanh(h)) * weighted
            parts = [terms[k : k + 16, :] for k in range(0, n, 16)]
            while len(parts) > 1:
                parts = [sum(parts[k + 1 : k + 2], parts[k]) for k in range(0, len(parts), 2)]
            total = jnp.sum(parts[0].astype(F32), axis=0, keepdims=True)
            spot = pl.ds(fr * nat + local, 1)
            if add:
                msg_s[spot, :] = msg_s[spot, :] + total
            else:
                msg_s[spot, :] = total

    def sweep(l, n, offset, first_id, load_feat, add):
        def step(k, _):
            for j in range(UNROLL):
                atom(l, k * UNROLL + j, n, offset, first_id, load_feat, add)
            return 0

        lax.fori_loop(0, block_atoms // UNROLL, step, 0)

    for l in range(per):
        base = own_base(l)
        sweep(l, own_n[l], 0, base, lambda l=l, base=base: feat[pl.ds(base, own_n[l]), :], False)

    halo.wait()
    for l in range(per):
        if ghost_n[l] == 0:
            continue
        base = ghost_base(l)
        fill(l, gs[l], ghost_buf[pl.ds(base, ghost_n[l]), width : width + 128], atoms)
        sweep(
            l, ghost_n[l], atoms, atoms + side * cap + base,
            lambda l=l, base=base: ghost_buf[pl.ds(base, ghost_n[l]), 0:width], True,
        )

    for copy in weight_copies:
        copy.wait()
    message = (msg_s[...] * message_scale).astype(BF16)
    hidden = silu(dot(message, w_msg[...])).astype(BF16)
    own = feat[pl.ds(pl.multiple_of(first, 16), nat), :].astype(F32)
    updated = (jnp.concatenate([own] * F, axis=0) + dot(hidden, w_upd[...])).astype(BF16)
    readout = silu(dot(updated, w_read[...])).astype(BF16)
    heads = lax.dot_general(w_heads[...], readout, (((1,), (1,)), ((), ())), preferred_element_type=F32)
    segment = lane1 // nat
    z_s[...] = jnp.zeros_like(z_s)
    for cc in range(3):
        total = jnp.zeros((1, 128), F32)
        for a in range(3):
            rot = jnp.zeros((1, 128), F32)
            for fr in range(F):
                rot = jnp.where(segment == fr, fr_s[fr, a : a + 1, cc : cc + 1], rot)
            total = total + rot * heads[a : a + 1, :]
        z_s[cc : cc + 1, :] = total
    z_s[3:4, :] = heads[3:4, :]
    z = z_s[...]
    total = z
    for k in range(1, F):
        total = total + pltpu.roll(z, k * nat, 1)
    fin_stage[...] = jnp.where(segment == f, total / F, 0.0)
    fin_copies = [
        pltpu.make_async_remote_copy(
            src_ref=fin_stage, dst_ref=fin_s.at[k], send_sem=fin_send.at[k], recv_sem=fin_recv.at[k],
            device_id={"frame": peer}, device_id_type=MESH,
        )
        for k, peer in enumerate(peers)
    ]
    for copy in fin_copies:
        copy.start()
    result = fin_stage[...]
    for k, copy in enumerate(fin_copies):
        copy.wait()
        result = result + fin_s[k]
    out[...] = result[0:4, :]


def local(F, D, features, positions, neighbours, counts, send_rows, frames, w_edge, b_edge,
          w_message, w_update, w_readout, w_heads):
    atoms, width = features.shape
    cap = send_rows.shape[2]
    slots = neighbours.shape[1]
    per = atoms // block_atoms // F
    vmem = pl.BlockSpec(memory_space=pltpu.VMEM)
    hbm = pl.BlockSpec(memory_space=pl.ANY)
    dma = pltpu.SemaphoreType.DMA
    return pl.pallas_call(
        functools.partial(kernel, F, D, atoms, cap, width),
        out_shape=jax.ShapeDtypeStruct((4, atoms), F32),
        in_specs=[vmem] * 8 + [hbm] * 3 + [vmem],
        out_specs=vmem,
        scratch_shapes=[
            pltpu.VMEM((128, atoms), F32),
            pltpu.VMEM((8, 128), F32),
            pltpu.VMEM((atoms, slots), F32),
            pltpu.VMEM((atoms, 128), F32),
            pltpu.VMEM((atoms, 128), BF16),
            pltpu.VMEM((cap, width + 128), BF16),
            pltpu.VMEM((cap, width + 128), BF16),
            pltpu.VMEM((per * (atoms + cap), 256), BF16),
            pltpu.VMEM((8, 128), F32),
            pltpu.VMEM((F, 8, 128), F32),
            pltpu.VMEM((32, width), F32),
            pltpu.VMEM((256, F * width), BF16),
            pltpu.VMEM((F * per * block_atoms, width), F32),
            pltpu.VMEM((8, 128), F32),
            pltpu.VMEM((8, 128), F32),
            pltpu.VMEM((F, 8, 128), F32),
            pltpu.VMEM((width, width), BF16),
            pltpu.VMEM((width, width), BF16),
            pltpu.VMEM((width, width), BF16),
            dma((3,)),
            dma,
            dma,
            dma((F - 1,)),
            dma((F - 1,)),
            dma((F - 1,)),
            dma((F - 1,)),
        ],
        compiler_params=pltpu.CompilerParams(
            collective_id=0, has_side_effects=True, vmem_limit_bytes=48 * 1024 * 1024
        ),
    )(
        features, positions, neighbours, counts.reshape(1, -1), send_rows.reshape(2, cap),
        frames.transpose(1, 0, 2), w_edge, b_edge.reshape(1, -1), w_message, w_update, w_readout,
        w_heads.T,
    )


def solution(mesh):
    placed = (
        P("dom", None),
        P(None, "dom"),
        P("dom", None),
        P("dom"),
        P("dom", None, None),
        P("frame", None, None),
        P(),
        P(),
        P(),
        P(),
        P(),
        P(),
    )
    body = functools.partial(local, mesh.shape["frame"], mesh.shape["dom"])
    return jax.shard_map(
        body, mesh=mesh, in_specs=placed, out_specs=P(None, "dom"), check_vma=False
    )
```

```python
import functools

import jax
import jax.numpy as jnp
from jax import lax
from jax.experimental import pallas as pl
from jax.experimental.pallas import tpu as pltpu
from jax.sharding import PartitionSpec as P

F32 = jnp.float32
BF16 = jnp.bfloat16
MESH = pl.DeviceIdType.MESH
WINDOW = 128
message_scale = 0.0884
radial_step = 1.25
block_atoms = 16
ROWS = 512
COLS = 256


def iota(shape, dim):
    return lax.broadcasted_iota(jnp.int32, shape, dim)


def dot(a, b):
    return jnp.dot(a, b, preferred_element_type=F32)


def split(value):
    high = value.astype(BF16).astype(F32)
    return high, value - high


def silu(x):
    half = 0.5 * x
    return half + half * jnp.tanh(half)


def up16(n):
    return (n + 15) // 16 * 16


def chunk_sizes(F, atoms, cap):
    blocks = atoms // block_atoms
    per = blocks // F
    span = atoms + 2 * cap - WINDOW
    own, ghost = [0] * per, [0] * per
    for f in range(F):
        for b in range(f * per, (f + 1) * per):
            start = b * span // max(blocks - 1, 1)
            low, high = max(start - cap, 0), min(start + WINDOW - cap, atoms)
            below, above = max(cap - start, 0), max(start + WINDOW - cap - atoms, 0)
            if f < F // 2:
                assert above == 0
                l, need, gh = b - f * per, high, below
            else:
                assert below == 0
                l, need, gh = (f + 1) * per - 1 - b, atoms - low, above
            own[l] = max(own[l], up16(need))
            ghost[l] = max(ghost[l], up16(gh))
    return own, ghost


def kernel(
    F, D, atoms, cap, width,
    feat_h, pos_h, nbr_h, cnt_h, send_h, frames_h, w_edge_h, b_edge_h, w_msg_h, w_upd_h, w_read_h,
    w_heads_h,
    out,
    feat, pos, nbr, cnt, send, frames, w_edge, b_edge, w_heads,
    left_s, wgt_s, table, nbr_s, add_s, own_u, send_buf, ghost_buf, lhs, fr_stage, fr_s, base_s, wst,
    msg_s, z_s, fin_stage, fin_s, w_msg, w_upd, w_read,
    w_sem, halo_send, halo_recv, fr_send, fr_recv, fin_send, fin_recv,
):
    f = lax.axis_index("frame")
    d = lax.axis_index("dom")
    side = f // (F // 2)
    blocks = atoms // block_atoms
    per = blocks // F
    nat = per * block_atoms
    own_n, ghost_n = chunk_sizes(F, atoms, cap)
    region = atoms + cap
    first = f * nat

    barrier = pltpu.get_barrier_semaphore()
    peers = [lax.rem(f + k, F) for k in range(1, F)]
    up, down = lax.rem(d + 1, D), lax.rem(d + D - 1, D)
    for peer in peers:
        pl.semaphore_signal(barrier, inc=1, device_id={"frame": peer}, device_id_type=MESH)
    for near in (up, down):
        pl.semaphore_signal(barrier, inc=1, device_id={"dom": near}, device_id_type=MESH)
    moves = (
        (pos_h, pos), (cnt_h, cnt), (send_h, send), (feat_h, feat), (frames_h, frames),
        (nbr_h, nbr), (w_edge_h, w_edge), (b_edge_h, b_edge),
        (w_msg_h, w_msg), (w_upd_h, w_upd), (w_read_h, w_read), (w_heads_h, w_heads),
    )
    copies = [pltpu.make_async_copy(src, dst, w_sem.at[n]) for n, (src, dst) in enumerate(moves)]
    for copy in copies:
        copy.start()
    early, weight_copies = copies[:8], copies[8:]

    lane = iota((128, 128), 1)
    row = iota((128, 128), 0)

    for copy in early:
        copy.wait()
    table[...] = jnp.zeros_like(table)
    table[0:3, :] = pos[...].astype(F32)
    table[3:4, :] = cnt[...].astype(F32)
    by_atom = table[...].T
    sq = jnp.sum(jnp.where(lane < 3, by_atom * by_atom, 0.0), axis=1, keepdims=True)
    sq_hi, rest = split(sq)
    sq_mid, sq_lo = split(rest)
    u = jnp.where(lane < 3, by_atom, 0.0)
    u = jnp.where(lane == 3, sq_hi, u)
    u = jnp.where(lane == 4, sq_mid, u)
    u = jnp.where(lane == 5, sq_lo, u)
    u = jnp.where((lane >= 6) & (lane < 9), 1.0, u)
    own_u[...] = u.astype(BF16)

    fr_stage[...] = jnp.zeros_like(fr_stage)
    for a in range(3):
        fr_stage[a : a + 1, 0:3] = frames[a]
    fr_s[f] = fr_stage[...]
    chosen = jnp.where(side == 0, send[1:2, :], send[0:1, :])
    pick = (iota((atoms, cap), 0) == chosen).astype(F32).T.astype(BF16)
    send_buf[:, 0:width] = dot(pick, feat[...]).astype(BF16)
    send_buf[:, width : width + 128] = dot(pick, own_u[...]).astype(BF16)

    pl.semaphore_wait(barrier, F + 1)
    target = jnp.where(side == 0, up, down)
    halo = pltpu.make_async_remote_copy(
        src_ref=send_buf, dst_ref=ghost_buf, send_sem=halo_send, recv_sem=halo_recv,
        device_id={"dom": target}, device_id_type=MESH,
    )
    fr_copies = [
        pltpu.make_async_remote_copy(
            src_ref=fr_stage, dst_ref=fr_s.at[f], send_sem=fr_send.at[k], recv_sem=fr_recv.at[k],
            device_id={"frame": peer}, device_id_type=MESH,
        )
        for k, peer in enumerate(peers)
    ]
    for copy in fr_copies:
        copy.start()
    halo.start()

    live = iota((atoms, nbr.shape[1]), 1).astype(F32) < by_atom[:, 3:4]
    nbr_s[...] = jnp.where(live, nbr[...].astype(F32), -1.0)

    radial = lane % 8
    spot = (lane // 8) * 2 + radial - 6
    special = radial >= 6
    place = special & (spot < 6) & (row < 3) & (row == spot % 3)
    place_neg = special & (spot >= 6) & (spot < 12) & (row < 3) & (row == spot % 3)
    place_one = special & (spot >= 12) & (spot < 14) & (row == 6)
    place_add = jnp.where(place_one, 1.0, jnp.where(place_neg, -1.0, 0.0)).astype(BF16)
    add_s[...] = dot(own_u[...], place_add)
    place = jnp.where(place, 1.0, 0.0).astype(BF16)
    centres = radial[0:1, :].astype(F32) * radial_step

    def block_rows(l):
        return (l * (1 - side) + (per - 1 - l) * side) * block_atoms

    def own_base(l):
        return pl.multiple_of(side * (atoms - own_n[l]), 16)

    def ghost_base(l):
        return pl.multiple_of((1 - side) * (cap - ghost_n[l]), 16)

    def geometry(l):
        start = first + block_rows(l)
        expand = jnp.where(row == start + lane // 8, 1.0, 0.0).astype(BF16)
        centre = dot(table[0:16, :].astype(BF16), expand)
        sub = iota((16, 128), 0)
        sqi = jnp.sum(jnp.where(sub < 3, centre * centre, 0.0), axis=0, keepdims=True) + 0.25
        hi, tail = split(sqi)
        mid, lo = split(tail)
        g = jnp.where((row >= 3) & (row < 6), 1.0, 0.0)
        for c in range(3):
            g = jnp.where(row == c, -2.0 * centre[c : c + 1, :], g)
        for c, part in enumerate((hi, mid, lo)):
            g = jnp.where(row == 6 + c, part, g)
        return g.astype(BF16)

    def fill(l, g, rows_u, offset):
        n = rows_u.shape[0]
        d2 = dot(rows_u, g)
        placed = dot(rows_u, place)
        dist = jnp.sqrt(jnp.maximum(d2, 0.25))
        gap = dist - centres
        value = jnp.exp(-(gap * gap))
        spec = special[0:n, :]
        lhs[l * region + offset : l * region + offset + n, 0:128] = jnp.where(spec, 0.0, value).astype(BF16)
        lhs[l * region + offset : l * region + offset + n, 128:256] = jnp.where(spec, placed, value).astype(BF16)

    gs = []
    for l in range(per):
        g = geometry(l)
        gs.append(g)
        fill(l, g, own_u[pl.ds(own_base(l), own_n[l]), :], 0)

    r = iota((256, 32), 0)
    c = iota((256, 32), 1)
    rb = r % 8
    rs = (r % 128) // 8 * 2 + rb - 6
    second = r // 128
    want = jnp.where(rb < 6, second * 6 + rb, -1)
    sp = (rb >= 6) & (second == 1)
    want = jnp.where(sp & (rs < 3), 12 + rs, want)
    want = jnp.where(sp & (rs >= 3) & (rs < 6), 12 + rs, want)
    want = jnp.where(sp & (rs >= 6) & (rs < 12), 6 + rs, want)
    want = jnp.where(sp & (rs >= 12) & (rs < 14), 6 + rs, want)
    sel = jnp.where(want == c, 1.0, 0.0).astype(BF16)
    base_s[...] = jnp.zeros_like(base_s)
    hi, lo = split(0.5 * w_edge[0:6, :])
    base_s[0:6, :] = hi
    base_s[6:12, :] = lo
    hi, lo = split(0.5 * b_edge[...])
    base_s[18:19, :] = hi
    base_s[19:20, :] = lo
    for copy in fr_copies:
        copy.wait()
    for fr in range(F):
        for cc in range(3):
            acc = fr_s[fr, 0:1, cc : cc + 1] * w_edge[6:7, :]
            acc = acc + fr_s[fr, 1:2, cc : cc + 1] * w_edge[7:8, :]
            acc = acc + fr_s[fr, 2:3, cc : cc + 1] * w_edge[8:9, :]
            hi, lo = split(0.5 * acc)
            base_s[12 + cc : 13 + cc, :] = hi
            base_s[15 + cc : 16 + cc, :] = lo
        wst[:, fr * width : (fr + 1) * width] = dot(sel, base_s[...].astype(BF16)).astype(BF16)

    lane1 = iota((1, 128), 1)
    group = lane1 // 8
    special1 = lane1 % 8 >= 6

    def sweep(l, n, offset, first_id, load_feat, add):
        many = max(k for k in (1, 2, 4, 8, 16) if k * n <= ROWS)

        def step(k, _):
            ids = (first_id + iota((n, 128), 0)).astype(F32)
            for j in range(many):
                i = k * many + j
                own_row = pl.ds(first + block_rows(l) + i, 1)
                mult = jnp.sum(jnp.where(ids == nbr_s[own_row, :], 1.0, 0.0), axis=1, keepdims=True)
                wgt_s[j * n : (j + 1) * n, :] = load_feat() * mult.astype(BF16)
                mask = jnp.where((group == i) & (~special1), 1.0, 0.0)
                left1 = lhs[l * region + offset : l * region + offset + n, 0:128] * mask.astype(BF16)
                left2 = lhs[l * region + offset : l * region + offset + n, 128:256]
                left2 = left2 * jnp.where(special1, 1.0, mask).astype(BF16) + add_s[own_row, :].astype(BF16)
                left_s[j * n : (j + 1) * n, 0:128] = left1
                left_s[j * n : (j + 1) * n, 128:256] = left2
            for c in range(F * width // COLS):
                fr, lanes = divmod(c * COLS, width)
                h = dot(left_s[0 : many * n, :], wst[:, c * COLS : (c + 1) * COLS]).astype(BF16)
                terms = (h + h * jnp.tanh(h)) * wgt_s[0 : many * n, lanes : lanes + COLS]
                for j in range(many):
                    parts = [terms[j * n + r : j * n + r + 16, :] for r in range(0, n, 16)]
                    while len(parts) > 1:
                        parts = [sum(parts[r + 1 : r + 2], parts[r]) for r in range(0, len(parts), 2)]
                    total = jnp.sum(parts[0].astype(F32), axis=0, keepdims=True)
                    spot = pl.ds(fr * nat + block_rows(l) + k * many + j, 1)
                    if add:
                        msg_s[spot, lanes : lanes + COLS] = msg_s[spot, lanes : lanes + COLS] + total
                    else:
                        msg_s[spot, lanes : lanes + COLS] = total
            return 0

        lax.fori_loop(0, block_atoms // many, step, 0)

    for l in range(per):
        base = own_base(l)
        sweep(l, own_n[l], 0, base, lambda l=l, base=base: feat[pl.ds(base, own_n[l]), :], False)

    halo.wait()
    for l in range(per):
        if ghost_n[l] == 0:
            continue
        base = ghost_base(l)
        fill(l, gs[l], ghost_buf[pl.ds(base, ghost_n[l]), width : width + 128], atoms)
        sweep(
            l, ghost_n[l], atoms, atoms + side * cap + base,
            lambda l=l, base=base: ghost_buf[pl.ds(base, ghost_n[l]), 0:width], True,
        )

    for copy in weight_copies:
        copy.wait()
    message = (msg_s[...] * message_scale).astype(BF16)
    hidden = silu(dot(message, w_msg[...])).astype(BF16)
    own = feat[pl.ds(pl.multiple_of(first, 16), nat), :].astype(F32)
    updated = (jnp.concatenate([own] * F, axis=0) + dot(hidden, w_upd[...])).astype(BF16)
    readout = silu(dot(updated, w_read[...])).astype(BF16)
    heads = lax.dot_general(w_heads[...], readout, (((1,), (1,)), ((), ())), preferred_element_type=F32)
    segment = lane1 // nat
    z_s[...] = jnp.zeros_like(z_s)
    for cc in range(3):
        total = jnp.zeros((1, 128), F32)
        for a in range(3):
            rot = jnp.zeros((1, 128), F32)
            for fr in range(F):
                rot = jnp.where(segment == fr, fr_s[fr, a : a + 1, cc : cc + 1], rot)
            total = total + rot * heads[a : a + 1, :]
        z_s[cc : cc + 1, :] = total
    z_s[3:4, :] = heads[3:4, :]
    z = z_s[...]
    total = z
    for k in range(1, F):
        total = total + pltpu.roll(z, k * nat, 1)
    fin_stage[...] = jnp.where(segment == f, total / F, 0.0)
    fin_copies = [
        pltpu.make_async_remote_copy(
            src_ref=fin_stage, dst_ref=fin_s.at[k], send_sem=fin_send.at[k], recv_sem=fin_recv.at[k],
            device_id={"frame": peer}, device_id_type=MESH,
        )
        for k, peer in enumerate(peers)
    ]
    for copy in fin_copies:
        copy.start()
    result = fin_stage[...]
    for k, copy in enumerate(fin_copies):
        copy.wait()
        result = result + fin_s[k]
    out[...] = result[0:4, :]


def local(F, D, features, positions, neighbours, counts, send_rows, frames, w_edge, b_edge,
          w_message, w_update, w_readout, w_heads):
    atoms, width = features.shape
    cap = send_rows.shape[2]
    slots = neighbours.shape[1]
    per = atoms // block_atoms // F
    vmem = pl.BlockSpec(memory_space=pltpu.VMEM)
    hbm = pl.BlockSpec(memory_space=pltpu.HBM)
    dma = pltpu.SemaphoreType.DMA
    return pl.pallas_call(
        functools.partial(kernel, F, D, atoms, cap, width),
        out_shape=jax.ShapeDtypeStruct((4, atoms), F32),
        in_specs=[hbm] * 12,
        out_specs=vmem,
        scratch_shapes=[
            pltpu.VMEM((atoms, width), BF16),
            pltpu.VMEM((3, atoms), BF16),
            pltpu.VMEM((atoms, slots), jnp.int32),
            pltpu.VMEM((1, atoms), jnp.int32),
            pltpu.VMEM((2, cap), jnp.int32),
            pltpu.VMEM((3, 1, 3), F32),
            pltpu.VMEM((w_edge.shape[0], width), F32),
            pltpu.VMEM((1, width), F32),
            pltpu.VMEM((4, width), BF16),
            pltpu.VMEM((ROWS, 256), BF16),
            pltpu.VMEM((ROWS, width), BF16),
            pltpu.VMEM((128, atoms), F32),
            pltpu.VMEM((atoms, slots), F32),
            pltpu.VMEM((atoms, 128), F32),
            pltpu.VMEM((atoms, 128), BF16),
            pltpu.VMEM((cap, width + 128), BF16),
            pltpu.VMEM((cap, width + 128), BF16),
            pltpu.VMEM((per * (atoms + cap), 256), BF16),
            pltpu.VMEM((8, 128), F32),
            pltpu.VMEM((F, 8, 128), F32),
            pltpu.VMEM((32, width), F32),
            pltpu.VMEM((256, F * width), BF16),
            pltpu.VMEM((F * per * block_atoms, width), F32),
            pltpu.VMEM((8, 128), F32),
            pltpu.VMEM((8, 128), F32),
            pltpu.VMEM((F, 8, 128), F32),
            pltpu.VMEM((width, width), BF16),
            pltpu.VMEM((width, width), BF16),
            pltpu.VMEM((width, width), BF16),
            dma((12,)),
            dma,
            dma,
            dma((F - 1,)),
            dma((F - 1,)),
            dma((F - 1,)),
            dma((F - 1,)),
        ],
        compiler_params=pltpu.CompilerParams(
            collective_id=0, has_side_effects=True, vmem_limit_bytes=63 * 1024 * 1024
        ),
    )(
        features, positions, neighbours, counts.reshape(1, -1), send_rows.reshape(2, cap),
        frames.transpose(1, 0, 2), w_edge, b_edge.reshape(1, -1), w_message, w_update, w_readout,
        w_heads.T,
    )


def solution(mesh):
    placed = (
        P("dom", None),
        P(None, "dom"),
        P("dom", None),
        P("dom"),
        P("dom", None, None),
        P("frame", None, None),
        P(),
        P(),
        P(),
        P(),
        P(),
        P(),
    )
    body = functools.partial(local, mesh.shape["frame"], mesh.shape["dom"])
    return jax.shard_map(
        body, mesh=mesh, in_specs=placed, out_specs=P(None, "dom"), check_vma=False
    )
```

```python
import functools

import jax
import jax.numpy as jnp
from jax import lax
from jax.experimental import pallas as pl
from jax.experimental.pallas import tpu as pltpu
from jax.sharding import PartitionSpec as P

F32 = jnp.float32
BF16 = jnp.bfloat16
MESH = pl.DeviceIdType.MESH
WINDOW = 128
message_scale = 0.0884
radial_step = 1.25
block_atoms = 16
ROWS = 512
COLS = 256


def iota(shape, dim):
    return lax.broadcasted_iota(jnp.int32, shape, dim)


def dot(a, b):
    return jnp.dot(a, b, preferred_element_type=F32)


def split(value):
    high = value.astype(BF16).astype(F32)
    return high, value - high


def silu(x):
    half = 0.5 * x
    return half + half * jnp.tanh(half)


def up16(n):
    return (n + 15) // 16 * 16


def chunk_sizes(F, atoms, cap):
    blocks = atoms // block_atoms
    per = blocks // F
    span = atoms + 2 * cap - WINDOW
    own, ghost = [0] * per, [0] * per
    for f in range(F):
        for b in range(f * per, (f + 1) * per):
            start = b * span // max(blocks - 1, 1)
            low, high = max(start - cap, 0), min(start + WINDOW - cap, atoms)
            below, above = max(cap - start, 0), max(start + WINDOW - cap - atoms, 0)
            if f < F // 2:
                assert above == 0
                l, need, gh = b - f * per, high, below
            else:
                assert below == 0
                l, need, gh = (f + 1) * per - 1 - b, atoms - low, above
            own[l] = max(own[l], up16(need))
            ghost[l] = max(ghost[l], up16(gh))
    return own, ghost


def kernel(
    F, D, atoms, cap, width,
    feat_h, pos_h, nbr_h, cnt_h, send_h, frames_h, w_edge_h, b_edge_h, w_msg_h, w_upd_h, w_read_h,
    w_heads_h,
    out,
    feat, pos, nbr, cnt, send, frames, w_edge, b_edge, w_heads,
    left_s, wgt_s, table, nbr_s, add_s, own_u, send_buf, ghost_buf, lhs, fr_stage, fr_s, base_s, wst,
    msg_s, z_s, fin_stage, fin_s, w_msg, w_upd, w_read,
    w_sem, halo_send, halo_recv, fr_send, fr_recv, fin_send, fin_recv,
):
    f = lax.axis_index("frame")
    d = lax.axis_index("dom")
    side = f // (F // 2)
    blocks = atoms // block_atoms
    per = blocks // F
    nat = per * block_atoms
    own_n, ghost_n = chunk_sizes(F, atoms, cap)
    region = atoms + cap
    first = f * nat

    barrier = pltpu.get_barrier_semaphore()
    peers = [lax.rem(f + k, F) for k in range(1, F)]
    up, down = lax.rem(d + 1, D), lax.rem(d + D - 1, D)
    for peer in peers:
        pl.semaphore_signal(barrier, inc=1, device_id={"frame": peer}, device_id_type=MESH)
    for near in (up, down):
        pl.semaphore_signal(barrier, inc=1, device_id={"dom": near}, device_id_type=MESH)
    moves = (
        (pos_h, pos), (cnt_h, cnt), (send_h, send), (feat_h, feat), (frames_h, frames),
        (nbr_h, nbr), (w_edge_h, w_edge), (b_edge_h, b_edge),
        (w_msg_h, w_msg), (w_upd_h, w_upd), (w_read_h, w_read), (w_heads_h, w_heads),
    )
    copies = [pltpu.make_async_copy(src, dst, w_sem.at[n]) for n, (src, dst) in enumerate(moves)]
    for copy in copies:
        copy.start()
    weight_copies = copies[8:]

    lane = iota((128, 128), 1)
    row = iota((128, 128), 0)
    lane1 = iota((1, 128), 1)
    group = lane1 >> 3
    radial = lane1 & 7
    special1 = radial >= 6

    copies[0].wait()
    copies[1].wait()
    table[...] = jnp.zeros_like(table)
    table[0:3, :] = pos[...].astype(F32)
    table[3:4, :] = cnt[...].astype(F32)
    by_atom = table[...].T
    sq = jnp.sum(jnp.where(lane < 3, by_atom * by_atom, 0.0), axis=1, keepdims=True)
    sq_hi, rest = split(sq)
    sq_mid, sq_lo = split(rest)
    u = jnp.where(lane < 3, by_atom, 0.0)
    u = jnp.where(lane == 3, sq_hi, u)
    u = jnp.where(lane == 4, sq_mid, u)
    u = jnp.where(lane == 5, sq_lo, u)
    u = jnp.where((lane >= 6) & (lane < 9), 1.0, u)
    own_u[...] = u.astype(BF16)

    copies[4].wait()
    fr_stage[...] = jnp.zeros_like(fr_stage)
    for a in range(3):
        fr_stage[a : a + 1, 0:3] = frames[a]
    fr_s[0] = fr_stage[...]
    copies[2].wait()
    copies[3].wait()
    chosen = jnp.where(side == 0, send[1:2, :], send[0:1, :])
    pick = (iota((atoms, cap), 0) == chosen).astype(F32).T.astype(BF16)
    send_buf[:, 0:width] = dot(pick, feat[...]).astype(BF16)
    send_buf[:, width : width + 128] = dot(pick, own_u[...]).astype(BF16)
    halo = pltpu.make_async_remote_copy(
        src_ref=send_buf, dst_ref=ghost_buf, send_sem=halo_send, recv_sem=halo_recv,
        device_id={"dom": jnp.where(side == 0, up, down)}, device_id_type=MESH,
    )
    fr_copies = [
        pltpu.make_async_remote_copy(
            src_ref=fr_stage, dst_ref=fr_s.at[F - k], send_sem=fr_send.at[k - 1],
            recv_sem=fr_recv.at[F - k - 1], device_id={"frame": peers[k - 1]}, device_id_type=MESH,
        )
        for k in range(1, F)
    ]

    copies[5].wait()
    live = iota((atoms, nbr.shape[1]), 1).astype(F32) < by_atom[:, 3:4]
    nbr_s[...] = jnp.where(live, nbr[...].astype(F32), -1.0)

    spot = jnp.where(special1, group * 2 + radial - 6, -1)
    place_row = jnp.where(spot < 3, spot, jnp.where(spot < 6, spot - 3, -1))
    neg_row = jnp.where((spot >= 6) & (spot < 9), spot - 6, -1)
    neg_row = jnp.where((spot >= 9) & (spot < 12), spot - 9, neg_row)
    one_row = jnp.where((spot >= 12) & (spot < 14), 6, -1)
    place_add = jnp.where(row == one_row, 1.0, jnp.where(row == neg_row, -1.0, 0.0)).astype(BF16)
    add_s[...] = dot(own_u[...], place_add)
    place = jnp.where(row == place_row, 1.0, 0.0).astype(BF16)
    centres = radial.astype(F32) * radial_step

    def block_rows(l):
        return (l * (1 - side) + (per - 1 - l) * side) * block_atoms

    def own_base(l):
        return pl.multiple_of(side * (atoms - own_n[l]), 16)

    def ghost_base(l):
        return pl.multiple_of((1 - side) * (cap - ghost_n[l]), 16)

    def geometry(l):
        start = first + block_rows(l)
        expand = jnp.where(row == start + group, 1.0, 0.0).astype(BF16)
        centre = dot(table[0:16, :].astype(BF16), expand)
        sub = iota((16, 128), 0)
        sqi = jnp.sum(jnp.where(sub < 3, centre * centre, 0.0), axis=0, keepdims=True) + 0.25
        hi, tail = split(sqi)
        mid, lo = split(tail)
        g = jnp.where(sub < 3, -2.0 * centre, jnp.where(sub < 6, 1.0, 0.0))
        for c, part in enumerate((hi, mid, lo)):
            g = jnp.where(sub == 6 + c, part, g)
        g = jnp.concatenate([g.astype(BF16), jnp.zeros((112, 128), BF16)], axis=0)
        return jnp.concatenate([g, place], axis=1)

    def fill(l, g, rows_u, offset):
        n = rows_u.shape[0]
        both = dot(rows_u, g)
        d2, placed = both[:, 0:128], both[:, 128:256]
        dist = jnp.sqrt(jnp.maximum(d2, 0.25))
        gap = dist - centres
        value = jnp.exp(-(gap * gap))
        at = l * region + offset
        lhs[at : at + n, 0:128] = jnp.where(special1, 0.0, value).astype(BF16)
        lhs[at : at + n, 128:256] = jnp.where(special1, placed, value).astype(BF16)

    gs = []
    for l in range(per):
        g = geometry(l)
        gs.append(g)
        fill(l, g, own_u[pl.ds(own_base(l), own_n[l]), :], 0)

    def wanted(second):
        want = jnp.where(special1, -1, radial + 6 * second)
        if second:
            want = jnp.where((spot >= 0) & (spot < 6), spot + 12, want)
            want = jnp.where((spot >= 6) & (spot < 14), spot + 6, want)
        return jnp.where(iota((32, 128), 0) == want, 1.0, 0.0).T.astype(BF16)

    sel = jnp.concatenate([wanted(0), wanted(1)], axis=0)
    copies[6].wait()
    copies[7].wait()
    base_s[...] = jnp.zeros_like(base_s)
    hi, lo = split(0.5 * w_edge[0:6, :])
    base_s[0:6, :] = hi
    base_s[6:12, :] = lo
    hi, lo = split(0.5 * b_edge[...])
    base_s[18:19, :] = hi
    base_s[19:20, :] = lo

    def edge_weights(fr):
        for cc in range(3):
            acc = fr_s[fr, 0:1, cc : cc + 1] * w_edge[6:7, :]
            acc = acc + fr_s[fr, 1:2, cc : cc + 1] * w_edge[7:8, :]
            acc = acc + fr_s[fr, 2:3, cc : cc + 1] * w_edge[8:9, :]
            hi, lo = split(0.5 * acc)
            base_s[12 + cc : 13 + cc, :] = hi
            base_s[15 + cc : 16 + cc, :] = lo
        wst[:, fr * width : (fr + 1) * width] = dot(sel, base_s[...].astype(BF16)).astype(BF16)

    edge_weights(0)

    own_at = [block_atoms * sum(own_n[:l]) for l in range(per)]
    ghost_at = [block_atoms * (sum(own_n) + sum(ghost_n[:l])) for l in range(per)]

    def sweep(l, n, at, offset, first_id, load_feat, build, slots, add):
        many = max(k for k in (1, 2, 4, 8, 16) if k * n <= ROWS)

        def step(k, _):
            ids = (first_id + iota((n, 128), 0)).astype(F32)
            here = pl.multiple_of(at + k * (many * n), 16)
            for j in range(many if build else 0):
                i = k * many + j
                rows = pl.ds(pl.multiple_of(here + j * n, 16), n)
                own_row = pl.ds(first + block_rows(l) + i, 1)
                mult = jnp.sum(jnp.where(ids == nbr_s[own_row, :], 1.0, 0.0), axis=1, keepdims=True)
                wgt_s[rows, :] = load_feat() * mult.astype(BF16)
                mask = jnp.where((group == i) & (~special1), 1.0, 0.0)
                left1 = lhs[l * region + offset : l * region + offset + n, 0:128] * mask.astype(BF16)
                left2 = lhs[l * region + offset : l * region + offset + n, 128:256]
                left2 = left2 * jnp.where(special1, 1.0, mask).astype(BF16) + add_s[own_row, :].astype(BF16)
                left_s[rows, 0:128] = left1
                left_s[rows, 128:256] = left2
            for fr in slots:
                for lanes in range(0, width, COLS):
                    c = fr * width + lanes
                    h = dot(left_s[pl.ds(here, many * n), :], wst[:, c : c + COLS]).astype(BF16)
                    terms = (h + h * jnp.tanh(h)) * wgt_s[pl.ds(here, many * n), lanes : lanes + COLS]
                    for j in range(many):
                        parts = [terms[j * n + r : j * n + r + 16, :] for r in range(0, n, 16)]
                        while len(parts) > 1:
                            parts = [sum(parts[r + 1 : r + 2], parts[r]) for r in range(0, len(parts), 2)]
                        total = jnp.sum(parts[0].astype(F32), axis=0, keepdims=True)
                        spot = pl.ds(fr * nat + block_rows(l) + k * many + j, 1)
                        if add:
                            total = total + msg_s[spot, lanes : lanes + COLS]
                        msg_s[spot, lanes : lanes + COLS] = total
            return 0

        lax.fori_loop(0, block_atoms // many, step, 0)

    def own_sweep(l, build, slots):
        base = own_base(l)
        sweep(
            l, own_n[l], own_at[l], 0, base, lambda: feat[pl.ds(base, own_n[l]), :], build, slots, False
        )

    order = list(range(per))
    for l in order[:-1]:
        own_sweep(l, True, [0])
    pl.semaphore_wait(barrier, F + 1)
    for copy in fr_copies:
        copy.start()
    halo.start()
    own_sweep(order[-1], True, [0])
    for copy in fr_copies:
        copy.wait()
    for k in range(1, F):
        edge_weights(k)
    for l in order:
        own_sweep(l, False, list(range(1, F)))

    halo.wait()
    for l in range(per):
        if ghost_n[l] == 0:
            continue
        base = ghost_base(l)
        fill(l, gs[l], ghost_buf[pl.ds(base, ghost_n[l]), width : width + 128], atoms)
        sweep(
            l, ghost_n[l], ghost_at[l], atoms, atoms + side * cap + base,
            lambda l=l, base=base: ghost_buf[pl.ds(base, ghost_n[l]), 0:width], True,
            list(range(F)), True,
        )

    for copy in weight_copies:
        copy.wait()
    message = (msg_s[...] * message_scale).astype(BF16)
    hidden = silu(dot(message, w_msg[...])).astype(BF16)
    own = feat[pl.ds(pl.multiple_of(first, 16), nat), :].astype(F32)
    updated = (jnp.concatenate([own] * F, axis=0) + dot(hidden, w_upd[...])).astype(BF16)
    readout = silu(dot(updated, w_read[...])).astype(BF16)
    heads = lax.dot_general(w_heads[...], readout, (((1,), (1,)), ((), ())), preferred_element_type=F32)
    segment = lane1 // nat
    z_s[...] = jnp.zeros_like(z_s)
    for cc in range(3):
        total = jnp.zeros((1, 128), F32)
        for a in range(3):
            rot = jnp.zeros((1, 128), F32)
            for fr in range(F):
                rot = jnp.where(segment == fr, fr_s[fr, a : a + 1, cc : cc + 1], rot)
            total = total + rot * heads[a : a + 1, :]
        z_s[cc : cc + 1, :] = total
    z_s[3:4, :] = heads[3:4, :]
    z = z_s[...]
    total = z
    for k in range(1, F):
        total = total + pltpu.roll(z, k * nat, 1)
    fin_stage[...] = jnp.where(segment == f, total / F, 0.0)
    fin_copies = [
        pltpu.make_async_remote_copy(
            src_ref=fin_stage, dst_ref=fin_s.at[k], send_sem=fin_send.at[k], recv_sem=fin_recv.at[k],
            device_id={"frame": peer}, device_id_type=MESH,
        )
        for k, peer in enumerate(peers)
    ]
    for copy in fin_copies:
        copy.start()
    result = fin_stage[...]
    for k, copy in enumerate(fin_copies):
        copy.wait()
        result = result + fin_s[k]
    out[...] = result[0:4, :]


def local(F, D, features, positions, neighbours, counts, send_rows, frames, w_edge, b_edge,
          w_message, w_update, w_readout, w_heads):
    atoms, width = features.shape
    cap = send_rows.shape[2]
    slots = neighbours.shape[1]
    per = atoms // block_atoms // F
    rows = block_atoms * sum(sum(sizes) for sizes in chunk_sizes(F, atoms, cap))
    vmem = pl.BlockSpec(memory_space=pltpu.VMEM)
    hbm = pl.BlockSpec(memory_space=pltpu.HBM)
    dma = pltpu.SemaphoreType.DMA
    return pl.pallas_call(
        functools.partial(kernel, F, D, atoms, cap, width),
        out_shape=jax.ShapeDtypeStruct((4, atoms), F32),
        in_specs=[hbm] * 12,
        out_specs=vmem,
        scratch_shapes=[
            pltpu.VMEM((atoms, width), BF16),
            pltpu.VMEM((3, atoms), BF16),
            pltpu.VMEM((atoms, slots), jnp.int32),
            pltpu.VMEM((1, atoms), jnp.int32),
            pltpu.VMEM((2, cap), jnp.int32),
            pltpu.VMEM((3, 1, 3), F32),
            pltpu.VMEM((w_edge.shape[0], width), F32),
            pltpu.VMEM((1, width), F32),
            pltpu.VMEM((4, width), BF16),
            pltpu.VMEM((rows, 256), BF16),
            pltpu.VMEM((rows, width), BF16),
            pltpu.VMEM((128, atoms), F32),
            pltpu.VMEM((atoms, slots), F32),
            pltpu.VMEM((atoms, 128), F32),
            pltpu.VMEM((atoms, 128), BF16),
            pltpu.VMEM((cap, width + 128), BF16),
            pltpu.VMEM((cap, width + 128), BF16),
            pltpu.VMEM((per * (atoms + cap), 256), BF16),
            pltpu.VMEM((8, 128), F32),
            pltpu.VMEM((F, 8, 128), F32),
            pltpu.VMEM((32, width), F32),
            pltpu.VMEM((256, F * width), BF16),
            pltpu.VMEM((F * per * block_atoms, width), F32),
            pltpu.VMEM((8, 128), F32),
            pltpu.VMEM((8, 128), F32),
            pltpu.VMEM((F, 8, 128), F32),
            pltpu.VMEM((width, width), BF16),
            pltpu.VMEM((width, width), BF16),
            pltpu.VMEM((width, width), BF16),
            dma((12,)),
            dma,
            dma,
            dma((F - 1,)),
            dma((F - 1,)),
            dma((F - 1,)),
            dma((F - 1,)),
        ],
        compiler_params=pltpu.CompilerParams(
            collective_id=0, has_side_effects=True, vmem_limit_bytes=63 * 1024 * 1024
        ),
    )(
        features, positions, neighbours, counts.reshape(1, -1), send_rows.reshape(2, cap),
        frames.transpose(1, 0, 2), w_edge, b_edge.reshape(1, -1), w_message, w_update, w_readout,
        w_heads.T,
    )


def solution(mesh):
    placed = (
        P("dom", None),
        P(None, "dom"),
        P("dom", None),
        P("dom"),
        P("dom", None, None),
        P("frame", None, None),
        P(),
        P(),
        P(),
        P(),
        P(),
        P(),
    )
    body = functools.partial(local, mesh.shape["frame"], mesh.shape["dom"])
    return jax.shard_map(
        body, mesh=mesh, in_specs=placed, out_specs=P(None, "dom"), check_vma=False
    )
```

```python
import functools

import jax
import jax.numpy as jnp
from jax import lax
from jax.experimental import pallas as pl
from jax.experimental.pallas import tpu as pltpu
from jax.sharding import PartitionSpec as P

F32 = jnp.float32
BF16 = jnp.bfloat16
MESH = pl.DeviceIdType.MESH
WINDOW = 128
message_scale = 0.0884
radial_step = 1.25
block_atoms = 16
ROWS = 2048
COLS = 256


def iota(shape, dim):
    return lax.broadcasted_iota(jnp.int32, shape, dim)


def dot(a, b):
    return jnp.dot(a, b, preferred_element_type=F32)


def split(value):
    high = value.astype(BF16).astype(F32)
    return high, value - high


def silu(x):
    half = 0.5 * x
    return half + half * jnp.tanh(half)


def up16(n):
    return (n + 15) // 16 * 16


def chunk_sizes(F, atoms, cap):
    blocks = atoms // block_atoms
    per = blocks // F
    span = atoms + 2 * cap - WINDOW
    own, ghost = [0] * per, [0] * per
    for f in range(F):
        for b in range(f * per, (f + 1) * per):
            start = b * span // max(blocks - 1, 1)
            low, high = max(start - cap, 0), min(start + WINDOW - cap, atoms)
            below, above = max(cap - start, 0), max(start + WINDOW - cap - atoms, 0)
            if f < F // 2:
                assert above == 0
                l, need, gh = b - f * per, high, below
            else:
                assert below == 0
                l, need, gh = (f + 1) * per - 1 - b, atoms - low, above
            own[l] = max(own[l], up16(need))
            ghost[l] = max(ghost[l], up16(gh))
    return own, ghost


def kernel(
    F, D, atoms, cap, width,
    feat_h, pos_h, nbr_h, cnt_h, send_h, frames_h, w_edge_h, b_edge_h, w_msg_h, w_upd_h, w_read_h,
    w_heads_h,
    out,
    feat, pos, nbr, cnt, send, frames, w_edge, b_edge, w_heads,
    left_s, wgt_s, table, nbr_s, add_s, own_u, send_buf, ghost_buf, lhs, fr_stage, fr_s, base_s, wst,
    msg_s, z_s, fin_stage, fin_s, w_msg, w_upd, w_read,
    w_sem, halo_send, halo_recv, fr_send, fr_recv, fin_send, fin_recv,
):
    f = lax.axis_index("frame")
    d = lax.axis_index("dom")
    side = f // (F // 2)
    blocks = atoms // block_atoms
    per = blocks // F
    nat = per * block_atoms
    own_n, ghost_n = chunk_sizes(F, atoms, cap)
    region = atoms + cap
    first = f * nat

    barrier = pltpu.get_barrier_semaphore()
    peers = [lax.rem(f + k, F) for k in range(1, F)]
    up, down = lax.rem(d + 1, D), lax.rem(d + D - 1, D)
    for peer in peers:
        pl.semaphore_signal(barrier, inc=1, device_id={"frame": peer}, device_id_type=MESH)
    for near in (up, down):
        pl.semaphore_signal(barrier, inc=1, device_id={"dom": near}, device_id_type=MESH)
    moves = (
        (pos_h, pos), (cnt_h, cnt), (send_h, send), (feat_h, feat), (frames_h, frames),
        (nbr_h, nbr), (w_edge_h, w_edge), (b_edge_h, b_edge),
        (w_msg_h, w_msg), (w_upd_h, w_upd), (w_read_h, w_read), (w_heads_h, w_heads),
    )
    copies = [pltpu.make_async_copy(src, dst, w_sem.at[n]) for n, (src, dst) in enumerate(moves)]
    for copy in copies:
        copy.start()
    weight_copies = copies[8:]

    lane = iota((128, 128), 1)
    row = iota((128, 128), 0)
    lane1 = iota((1, 128), 1)
    group = lane1 >> 3
    radial = lane1 & 7
    special1 = radial >= 6

    copies[0].wait()
    copies[1].wait()
    table[...] = jnp.zeros_like(table)
    table[0:3, :] = pos[...].astype(F32)
    table[3:4, :] = cnt[...].astype(F32)
    by_atom = table[...].T
    sq = jnp.sum(jnp.where(lane < 3, by_atom * by_atom, 0.0), axis=1, keepdims=True)
    sq_hi, rest = split(sq)
    sq_mid, sq_lo = split(rest)
    u = jnp.where(lane < 3, by_atom, 0.0)
    u = jnp.where(lane == 3, sq_hi, u)
    u = jnp.where(lane == 4, sq_mid, u)
    u = jnp.where(lane == 5, sq_lo, u)
    u = jnp.where((lane >= 6) & (lane < 9), 1.0, u)
    own_u[...] = u.astype(BF16)

    copies[4].wait()
    fr_stage[...] = jnp.zeros_like(fr_stage)
    for a in range(3):
        fr_stage[a : a + 1, 0:3] = frames[a]
    fr_s[0] = fr_stage[...]
    copies[2].wait()
    copies[3].wait()
    chosen = jnp.where(side == 0, send[1:2, :], send[0:1, :])
    pick = (iota((atoms, cap), 0) == chosen).astype(F32).T.astype(BF16)
    send_buf[:, 0:width] = dot(pick, feat[...]).astype(BF16)
    send_buf[:, width : width + 128] = dot(pick, own_u[...]).astype(BF16)
    halo = pltpu.make_async_remote_copy(
        src_ref=send_buf, dst_ref=ghost_buf, send_sem=halo_send, recv_sem=halo_recv,
        device_id={"dom": jnp.where(side == 0, up, down)}, device_id_type=MESH,
    )
    fr_copies = [
        pltpu.make_async_remote_copy(
            src_ref=fr_stage, dst_ref=fr_s.at[F - k], send_sem=fr_send.at[k - 1],
            recv_sem=fr_recv.at[F - k - 1], device_id={"frame": peers[k - 1]}, device_id_type=MESH,
        )
        for k in range(1, F)
    ]

    copies[5].wait()
    live = iota((atoms, nbr.shape[1]), 1).astype(F32) < by_atom[:, 3:4]
    nbr_s[...] = jnp.where(live, nbr[...].astype(F32), -1.0)

    spot = jnp.where(special1, group * 2 + radial - 6, -1)
    place_row = jnp.where(spot < 3, spot, jnp.where(spot < 6, spot - 3, -1))
    neg_row = jnp.where((spot >= 6) & (spot < 9), spot - 6, -1)
    neg_row = jnp.where((spot >= 9) & (spot < 12), spot - 9, neg_row)
    one_row = jnp.where((spot >= 12) & (spot < 14), 6, -1)
    place_add = jnp.where(row == one_row, 1.0, jnp.where(row == neg_row, -1.0, 0.0)).astype(BF16)
    add_s[...] = dot(own_u[...], place_add)
    place = jnp.where(row == place_row, 1.0, 0.0).astype(BF16)
    centres = radial.astype(F32) * radial_step

    def block_rows(l):
        return (l * (1 - side) + (per - 1 - l) * side) * block_atoms

    def own_base(l):
        return pl.multiple_of(side * (atoms - own_n[l]), 16)

    def ghost_base(l):
        return pl.multiple_of((1 - side) * (cap - ghost_n[l]), 16)

    def geometry(l):
        start = first + block_rows(l)
        expand = jnp.where(row == start + group, 1.0, 0.0).astype(BF16)
        centre = dot(table[0:16, :].astype(BF16), expand)
        sub = iota((16, 128), 0)
        sqi = jnp.sum(jnp.where(sub < 3, centre * centre, 0.0), axis=0, keepdims=True) + 0.25
        hi, tail = split(sqi)
        mid, lo = split(tail)
        g = jnp.where(sub < 3, -2.0 * centre, jnp.where(sub < 6, 1.0, 0.0))
        for c, part in enumerate((hi, mid, lo)):
            g = jnp.where(sub == 6 + c, part, g)
        g = jnp.concatenate([g.astype(BF16), jnp.zeros((112, 128), BF16)], axis=0)
        return jnp.concatenate([g, place], axis=1)

    def fill(l, g, rows_u, offset):
        n = rows_u.shape[0]
        both = dot(rows_u, g)
        d2, placed = both[:, 0:128], both[:, 128:256]
        dist = jnp.sqrt(jnp.maximum(d2, 0.25))
        gap = dist - centres
        value = jnp.exp(-(gap * gap))
        at = l * region + offset
        lhs[at : at + n, 0:128] = jnp.where(special1, 0.0, value).astype(BF16)
        lhs[at : at + n, 128:256] = jnp.where(special1, placed, value).astype(BF16)

    gs = []
    for l in range(per):
        g = geometry(l)
        gs.append(g)
        fill(l, g, own_u[pl.ds(own_base(l), own_n[l]), :], 0)

    def wanted(second):
        want = jnp.where(special1, -1, radial + 6 * second)
        if second:
            want = jnp.where((spot >= 0) & (spot < 6), spot + 12, want)
            want = jnp.where((spot >= 6) & (spot < 14), spot + 6, want)
        return jnp.where(iota((32, 128), 0) == want, 1.0, 0.0).T.astype(BF16)

    sel = jnp.concatenate([wanted(0), wanted(1)], axis=0)
    copies[6].wait()
    copies[7].wait()
    base_s[...] = jnp.zeros_like(base_s)
    hi, lo = split(0.5 * w_edge[0:6, :])
    base_s[0:6, :] = hi
    base_s[6:12, :] = lo
    hi, lo = split(0.5 * b_edge[...])
    base_s[18:19, :] = hi
    base_s[19:20, :] = lo

    def edge_weights(fr):
        for cc in range(3):
            acc = fr_s[fr, 0:1, cc : cc + 1] * w_edge[6:7, :]
            acc = acc + fr_s[fr, 1:2, cc : cc + 1] * w_edge[7:8, :]
            acc = acc + fr_s[fr, 2:3, cc : cc + 1] * w_edge[8:9, :]
            hi, lo = split(0.5 * acc)
            base_s[12 + cc : 13 + cc, :] = hi
            base_s[15 + cc : 16 + cc, :] = lo
        wst[:, fr * width : (fr + 1) * width] = dot(sel, base_s[...].astype(BF16)).astype(BF16)

    edge_weights(0)

    own_at = [block_atoms * sum(own_n[:l]) for l in range(per)]
    ghost_at = [block_atoms * (sum(own_n) + sum(ghost_n[:l])) for l in range(per)]

    def sweep(l, n, at, offset, first_id, load_feat, build, slots, add):
        many = max(k for k in (1, 2, 4, 8, 16) if k * n <= ROWS)

        def step(k, _):
            ids = (first_id + iota((n, 128), 0)).astype(F32)
            here = pl.multiple_of(at + k * (many * n), 16)
            for j in range(many if build else 0):
                i = k * many + j
                rows = pl.ds(pl.multiple_of(here + j * n, 16), n)
                own_row = pl.ds(first + block_rows(l) + i, 1)
                mult = jnp.sum(jnp.where(ids == nbr_s[own_row, :], 1.0, 0.0), axis=1, keepdims=True)
                wgt_s[rows, :] = load_feat() * mult.astype(BF16)
                mask = jnp.where((group == i) & (~special1), 1.0, 0.0)
                left1 = lhs[l * region + offset : l * region + offset + n, 0:128] * mask.astype(BF16)
                left2 = lhs[l * region + offset : l * region + offset + n, 128:256]
                left2 = left2 * jnp.where(special1, 1.0, mask).astype(BF16) + add_s[own_row, :].astype(BF16)
                left_s[rows, 0:128] = left1
                left_s[rows, 128:256] = left2
            for fr in slots:
                for lanes in range(0, width, COLS):
                    c = fr * width + lanes
                    h = dot(left_s[pl.ds(here, many * n), :], wst[:, c : c + COLS]).astype(BF16)
                    terms = (h + h * jnp.tanh(h)) * wgt_s[pl.ds(here, many * n), lanes : lanes + COLS]
                    for j in range(many):
                        parts = [terms[j * n + r : j * n + r + 16, :] for r in range(0, n, 16)]
                        while len(parts) > 1:
                            parts = [sum(parts[r + 1 : r + 2], parts[r]) for r in range(0, len(parts), 2)]
                        total = jnp.sum(parts[0].astype(F32), axis=0, keepdims=True)
                        spot = pl.ds(fr * nat + block_rows(l) + k * many + j, 1)
                        if add:
                            total = total + msg_s[spot, lanes : lanes + COLS]
                        msg_s[spot, lanes : lanes + COLS] = total
            return 0

        if many == block_atoms:
            step(0, 0)
        else:
            lax.fori_loop(0, block_atoms // many, step, 0)

    def own_sweep(l, build, slots):
        base = own_base(l)
        sweep(
            l, own_n[l], own_at[l], 0, base, lambda: feat[pl.ds(base, own_n[l]), :], build, slots, False
        )

    order = list(range(per))[::-1]
    own_sweep(order[0], True, [0])
    pl.semaphore_wait(barrier, F + 1)
    for copy in fr_copies:
        copy.start()
    halo.start()
    for l in order[1:2]:
        own_sweep(l, True, [0])
    for copy in fr_copies:
        copy.wait()
    for k in range(1, F):
        edge_weights(k)
    for l in order[:2]:
        own_sweep(l, False, list(range(1, F)))
    for l in order[2:]:
        own_sweep(l, True, list(range(F)))

    halo.wait()
    for l in range(per):
        if ghost_n[l] == 0:
            continue
        base = ghost_base(l)
        fill(l, gs[l], ghost_buf[pl.ds(base, ghost_n[l]), width : width + 128], atoms)
        sweep(
            l, ghost_n[l], ghost_at[l], atoms, atoms + side * cap + base,
            lambda l=l, base=base: ghost_buf[pl.ds(base, ghost_n[l]), 0:width], True,
            list(range(F)), True,
        )

    for copy in weight_copies:
        copy.wait()
    message = (msg_s[...] * message_scale).astype(BF16)
    hidden = silu(dot(message, w_msg[...])).astype(BF16)
    own = feat[pl.ds(pl.multiple_of(first, 16), nat), :].astype(F32)
    updated = (jnp.concatenate([own] * F, axis=0) + dot(hidden, w_upd[...])).astype(BF16)
    readout = silu(dot(updated, w_read[...])).astype(BF16)
    heads = lax.dot_general(w_heads[...], readout, (((1,), (1,)), ((), ())), preferred_element_type=F32)
    segment = lane1 // nat
    z_s[...] = jnp.zeros_like(z_s)
    for cc in range(3):
        total = jnp.zeros((1, 128), F32)
        for a in range(3):
            rot = jnp.zeros((1, 128), F32)
            for fr in range(F):
                rot = jnp.where(segment == fr, fr_s[fr, a : a + 1, cc : cc + 1], rot)
            total = total + rot * heads[a : a + 1, :]
        z_s[cc : cc + 1, :] = total
    z_s[3:4, :] = heads[3:4, :]
    z = z_s[...]
    total = z
    for k in range(1, F):
        total = total + pltpu.roll(z, k * nat, 1)
    fin_stage[...] = jnp.where(segment == f, total / F, 0.0)
    fin_copies = [
        pltpu.make_async_remote_copy(
            src_ref=fin_stage, dst_ref=fin_s.at[k], send_sem=fin_send.at[k], recv_sem=fin_recv.at[k],
            device_id={"frame": peer}, device_id_type=MESH,
        )
        for k, peer in enumerate(peers)
    ]
    for copy in fin_copies:
        copy.start()
    result = fin_stage[...]
    for k, copy in enumerate(fin_copies):
        copy.wait()
        result = result + fin_s[k]
    out[...] = result[0:4, :]


def local(F, D, features, positions, neighbours, counts, send_rows, frames, w_edge, b_edge,
          w_message, w_update, w_readout, w_heads):
    atoms, width = features.shape
    cap = send_rows.shape[2]
    slots = neighbours.shape[1]
    per = atoms // block_atoms // F
    rows = block_atoms * sum(sum(sizes) for sizes in chunk_sizes(F, atoms, cap))
    vmem = pl.BlockSpec(memory_space=pltpu.VMEM)
    hbm = pl.BlockSpec(memory_space=pltpu.HBM)
    dma = pltpu.SemaphoreType.DMA
    return pl.pallas_call(
        functools.partial(kernel, F, D, atoms, cap, width),
        out_shape=jax.ShapeDtypeStruct((4, atoms), F32),
        in_specs=[hbm] * 12,
        out_specs=vmem,
        scratch_shapes=[
            pltpu.VMEM((atoms, width), BF16),
            pltpu.VMEM((3, atoms), BF16),
            pltpu.VMEM((atoms, slots), jnp.int32),
            pltpu.VMEM((1, atoms), jnp.int32),
            pltpu.VMEM((2, cap), jnp.int32),
            pltpu.VMEM((3, 1, 3), F32),
            pltpu.VMEM((w_edge.shape[0], width), F32),
            pltpu.VMEM((1, width), F32),
            pltpu.VMEM((4, width), BF16),
            pltpu.VMEM((rows, 256), BF16),
            pltpu.VMEM((rows, width), BF16),
            pltpu.VMEM((128, atoms), F32),
            pltpu.VMEM((atoms, slots), F32),
            pltpu.VMEM((atoms, 128), F32),
            pltpu.VMEM((atoms, 128), BF16),
            pltpu.VMEM((cap, width + 128), BF16),
            pltpu.VMEM((cap, width + 128), BF16),
            pltpu.VMEM((per * (atoms + cap), 256), BF16),
            pltpu.VMEM((8, 128), F32),
            pltpu.VMEM((F, 8, 128), F32),
            pltpu.VMEM((32, width), F32),
            pltpu.VMEM((256, F * width), BF16),
            pltpu.VMEM((F * per * block_atoms, width), F32),
            pltpu.VMEM((8, 128), F32),
            pltpu.VMEM((8, 128), F32),
            pltpu.VMEM((F, 8, 128), F32),
            pltpu.VMEM((width, width), BF16),
            pltpu.VMEM((width, width), BF16),
            pltpu.VMEM((width, width), BF16),
            dma((12,)),
            dma,
            dma,
            dma((F - 1,)),
            dma((F - 1,)),
            dma((F - 1,)),
            dma((F - 1,)),
        ],
        compiler_params=pltpu.CompilerParams(
            collective_id=0, has_side_effects=True, vmem_limit_bytes=63 * 1024 * 1024
        ),
    )(
        features, positions, neighbours, counts.reshape(1, -1), send_rows.reshape(2, cap),
        frames.transpose(1, 0, 2), w_edge, b_edge.reshape(1, -1), w_message, w_update, w_readout,
        w_heads.T,
    )


def solution(mesh):
    placed = (
        P("dom", None),
        P(None, "dom"),
        P("dom", None),
        P("dom"),
        P("dom", None, None),
        P("frame", None, None),
        P(),
        P(),
        P(),
        P(),
        P(),
        P(),
    )
    body = functools.partial(local, mesh.shape["frame"], mesh.shape["dom"])
    return jax.shard_map(
        body, mesh=mesh, in_specs=placed, out_specs=P(None, "dom"), check_vma=False
    )
```

```python
import functools

import jax
import jax.numpy as jnp
from jax import lax
from jax.experimental import pallas as pl
from jax.experimental.pallas import tpu as pltpu
from jax.sharding import PartitionSpec as P

F32 = jnp.float32
BF16 = jnp.bfloat16
MESH = pl.DeviceIdType.MESH
WINDOW = 128
message_scale = 0.0884
radial_step = 1.25
block_atoms = 16
ROWS = 512
COLS = 256


def iota(shape, dim):
    return lax.broadcasted_iota(jnp.int32, shape, dim)


def dot(a, b):
    return jnp.dot(a, b, preferred_element_type=F32)


def split(value):
    high = value.astype(BF16).astype(F32)
    return high, value - high


def silu(x):
    half = 0.5 * x
    return half + half * jnp.tanh(half)


def up16(n):
    return (n + 15) // 16 * 16


def chunk_sizes(F, atoms, cap):
    blocks = atoms // block_atoms
    per = blocks // F
    span = atoms + 2 * cap - WINDOW
    own, ghost = [0] * per, [0] * per
    for f in range(F):
        for b in range(f * per, (f + 1) * per):
            start = b * span // max(blocks - 1, 1)
            low, high = max(start - cap, 0), min(start + WINDOW - cap, atoms)
            below, above = max(cap - start, 0), max(start + WINDOW - cap - atoms, 0)
            if f < F // 2:
                assert above == 0
                l, need, gh = b - f * per, high, below
            else:
                assert below == 0
                l, need, gh = (f + 1) * per - 1 - b, atoms - low, above
            own[l] = max(own[l], up16(need))
            ghost[l] = max(ghost[l], up16(gh))
    return own, ghost


def kernel(
    F, D, atoms, cap, width,
    feat_h, pos_h, nbr_h, cnt_h, send_h, frames_h, w_edge_h, b_edge_h, w_msg_h, w_upd_h, w_read_h,
    w_heads_h,
    out,
    feat, pos, nbr, cnt, send, frames, w_edge, b_edge, w_heads,
    left_s, wgt_s, table, nbr_s, add_s, own_u, send_buf, ghost_buf, lhs, fr_stage, fr_s, base_s, wst,
    msg_s, acc_s, z_s, fin_stage, fin_s, w_msg, w_upd, w_read,
    w_sem, halo_send, halo_recv, fr_send, fr_recv, fin_send, fin_recv,
):
    f = lax.axis_index("frame")
    d = lax.axis_index("dom")
    side = f // (F // 2)
    blocks = atoms // block_atoms
    per = blocks // F
    nat = per * block_atoms
    own_n, ghost_n = chunk_sizes(F, atoms, cap)
    region = atoms + cap
    first = f * nat

    barrier = pltpu.get_barrier_semaphore()
    peers = [lax.rem(f + k, F) for k in range(1, F)]
    up, down = lax.rem(d + 1, D), lax.rem(d + D - 1, D)
    for peer in peers:
        pl.semaphore_signal(barrier, inc=1, device_id={"frame": peer}, device_id_type=MESH)
    for near in (up, down):
        pl.semaphore_signal(barrier, inc=1, device_id={"dom": near}, device_id_type=MESH)
    moves = (
        (pos_h, pos), (cnt_h, cnt), (send_h, send), (feat_h, feat), (frames_h, frames),
        (nbr_h, nbr), (w_edge_h, w_edge), (b_edge_h, b_edge),
        (w_msg_h, w_msg), (w_upd_h, w_upd), (w_read_h, w_read), (w_heads_h, w_heads),
    )
    copies = [pltpu.make_async_copy(src, dst, w_sem.at[n]) for n, (src, dst) in enumerate(moves)]
    for copy in copies:
        copy.start()
    weight_copies = copies[8:]

    lane = iota((128, 128), 1)
    row = iota((128, 128), 0)
    lane1 = iota((1, 128), 1)
    group = lane1 >> 3
    radial = lane1 & 7
    special1 = radial >= 6

    copies[0].wait()
    copies[1].wait()
    table[...] = jnp.zeros_like(table)
    table[0:3, :] = pos[...].astype(F32)
    table[3:4, :] = cnt[...].astype(F32)
    by_atom = table[...].T
    sq = jnp.sum(jnp.where(lane < 3, by_atom * by_atom, 0.0), axis=1, keepdims=True)
    sq_hi, rest = split(sq)
    sq_mid, sq_lo = split(rest)
    u = jnp.where(lane < 3, by_atom, 0.0)
    u = jnp.where(lane == 3, sq_hi, u)
    u = jnp.where(lane == 4, sq_mid, u)
    u = jnp.where(lane == 5, sq_lo, u)
    u = jnp.where((lane >= 6) & (lane < 9), 1.0, u)
    own_u[...] = u.astype(BF16)

    copies[4].wait()
    fr_stage[...] = jnp.zeros_like(fr_stage)
    for a in range(3):
        fr_stage[a : a + 1, 0:3] = frames[a]
    fr_s[0] = fr_stage[...]
    copies[2].wait()
    copies[3].wait()
    chosen = jnp.where(side == 0, send[1:2, :], send[0:1, :])
    pick = (iota((atoms, cap), 0) == chosen).astype(F32).T.astype(BF16)
    send_buf[:, 0:width] = dot(pick, feat[...]).astype(BF16)
    send_buf[:, width : width + 128] = dot(pick, own_u[...]).astype(BF16)
    halo = pltpu.make_async_remote_copy(
        src_ref=send_buf, dst_ref=ghost_buf, send_sem=halo_send, recv_sem=halo_recv,
        device_id={"dom": jnp.where(side == 0, up, down)}, device_id_type=MESH,
    )
    fr_copies = [
        pltpu.make_async_remote_copy(
            src_ref=fr_stage, dst_ref=fr_s.at[F - k], send_sem=fr_send.at[k - 1],
            recv_sem=fr_recv.at[F - k - 1], device_id={"frame": peers[k - 1]}, device_id_type=MESH,
        )
        for k in range(1, F)
    ]

    copies[5].wait()
    live = iota((atoms, nbr.shape[1]), 1).astype(F32) < by_atom[:, 3:4]
    nbr_s[...] = jnp.where(live, nbr[...].astype(F32), -1.0)

    spot = jnp.where(special1, group * 2 + radial - 6, -1)
    place_row = jnp.where(spot < 3, spot, jnp.where(spot < 6, spot - 3, -1))
    neg_row = jnp.where((spot >= 6) & (spot < 9), spot - 6, -1)
    neg_row = jnp.where((spot >= 9) & (spot < 12), spot - 9, neg_row)
    one_row = jnp.where((spot >= 12) & (spot < 14), 6, -1)
    place_add = jnp.where(row == one_row, 1.0, jnp.where(row == neg_row, -1.0, 0.0)).astype(BF16)
    add_s[...] = dot(own_u[...], place_add)
    place = jnp.where(row == place_row, 1.0, 0.0).astype(BF16)
    centres = radial.astype(F32) * radial_step

    def block_rows(l):
        return (l * (1 - side) + (per - 1 - l) * side) * block_atoms

    def own_base(l):
        return pl.multiple_of(side * (atoms - own_n[l]), 16)

    def ghost_base(l):
        return pl.multiple_of((1 - side) * (cap - ghost_n[l]), 16)

    def geometry(l):
        start = first + block_rows(l)
        expand = jnp.where(row == start + group, 1.0, 0.0).astype(BF16)
        centre = dot(table[0:16, :].astype(BF16), expand)
        sub = iota((16, 128), 0)
        sqi = jnp.sum(jnp.where(sub < 3, centre * centre, 0.0), axis=0, keepdims=True) + 0.25
        hi, tail = split(sqi)
        mid, lo = split(tail)
        g = jnp.where(sub < 3, -2.0 * centre, jnp.where(sub < 6, 1.0, 0.0))
        for c, part in enumerate((hi, mid, lo)):
            g = jnp.where(sub == 6 + c, part, g)
        g = jnp.concatenate([g.astype(BF16), jnp.zeros((112, 128), BF16)], axis=0)
        return jnp.concatenate([g, place], axis=1)

    def fill(l, g, rows_u, offset):
        n = rows_u.shape[0]
        both = dot(rows_u, g)
        d2, placed = both[:, 0:128], both[:, 128:256]
        dist = jnp.sqrt(jnp.maximum(d2, 0.25))
        gap = dist - centres
        value = jnp.exp(-(gap * gap))
        at = l * region + offset
        lhs[at : at + n, 0:128] = jnp.where(special1, 0.0, value).astype(BF16)
        lhs[at : at + n, 128:256] = jnp.where(special1, placed, value).astype(BF16)

    gs = []
    for l in range(per):
        g = geometry(l)
        gs.append(g)
        fill(l, g, own_u[pl.ds(own_base(l), own_n[l]), :], 0)

    def wanted(second):
        want = jnp.where(special1, -1, radial + 6 * second)
        if second:
            want = jnp.where((spot >= 0) & (spot < 6), spot + 12, want)
            want = jnp.where((spot >= 6) & (spot < 14), spot + 6, want)
        return jnp.where(iota((32, 128), 0) == want, 1.0, 0.0).T.astype(BF16)

    sel = jnp.concatenate([wanted(0), wanted(1)], axis=0)
    copies[6].wait()
    copies[7].wait()
    base_s[...] = jnp.zeros_like(base_s)
    hi, lo = split(0.5 * w_edge[0:6, :])
    base_s[0:6, :] = hi
    base_s[6:12, :] = lo
    hi, lo = split(0.5 * b_edge[...])
    base_s[18:19, :] = hi
    base_s[19:20, :] = lo

    def edge_weights(fr):
        for cc in range(3):
            acc = fr_s[fr, 0:1, cc : cc + 1] * w_edge[6:7, :]
            acc = acc + fr_s[fr, 1:2, cc : cc + 1] * w_edge[7:8, :]
            acc = acc + fr_s[fr, 2:3, cc : cc + 1] * w_edge[8:9, :]
            hi, lo = split(0.5 * acc)
            base_s[12 + cc : 13 + cc, :] = hi
            base_s[15 + cc : 16 + cc, :] = lo
        wst[:, fr * width : (fr + 1) * width] = dot(sel, base_s[...].astype(BF16)).astype(BF16)

    edge_weights(0)

    own_at = [block_atoms * sum(own_n[:l]) for l in range(per)]
    ghost_at = [block_atoms * (sum(own_n) + sum(ghost_n[:l])) for l in range(per)]

    pending = []

    def flush():
        while pending:
            pending.pop()()

    def finish(h, at, n, atoms_here, fr, lanes, last):
        terms = (h + h * jnp.tanh(h)) * wgt_s[at : at + len(atoms_here) * n, lanes : lanes + COLS]
        for j, local in enumerate(atoms_here):
            parts = [terms[j * n + r : j * n + r + 16, :] for r in range(0, n, 16)]
            while len(parts) > 1:
                parts = [sum(parts[r + 1 : r + 2], parts[r]) for r in range(0, len(parts), 2)]
            total = parts[0].astype(F32)
            total = total[0:8, :] + total[8:16, :]
            eight = pl.ds(pl.multiple_of((fr * nat + local) * 8, 8), 8)
            if last:
                total = total + acc_s[eight, lanes : lanes + COLS]
                spot = pl.ds(fr * nat + local, 1)
                msg_s[spot, lanes : lanes + COLS] = jnp.sum(total, axis=0, keepdims=True)
            else:
                acc_s[eight, lanes : lanes + COLS] = total

    def sweep(l, n, at, offset, first_id, load_feat, build, slots, last):
        many = max(k for k in (1, 2, 4, 8, 16) if k * n <= ROWS)
        ids = (first_id + iota((n, 128), 0)).astype(F32)
        for k in range(0, block_atoms, many):
            here = at + k * n
            for i in range(k, k + many if build else k):
                rows = slice(at + i * n, at + i * n + n)
                own_row = pl.ds(first + block_rows(l) + i, 1)
                mult = jnp.sum(jnp.where(ids == nbr_s[own_row, :], 1.0, 0.0), axis=1, keepdims=True)
                wgt_s[rows, :] = load_feat() * mult.astype(BF16)
                mask = jnp.where((group == i) & (~special1), 1.0, 0.0)
                left1 = lhs[l * region + offset : l * region + offset + n, 0:128] * mask.astype(BF16)
                left2 = lhs[l * region + offset : l * region + offset + n, 128:256]
                left2 = left2 * jnp.where(special1, 1.0, mask).astype(BF16) + add_s[own_row, :].astype(BF16)
                left_s[rows, 0:128] = left1
                left_s[rows, 128:256] = left2
            atoms_here = [block_rows(l) + i for i in range(k, k + many)]
            for fr in slots:
                for lanes in range(0, width, COLS):
                    c = fr * width + lanes
                    h = dot(left_s[here : here + many * n, :], wst[:, c : c + COLS]).astype(BF16)
                    flush()
                    pending.append(functools.partial(finish, h, here, n, atoms_here, fr, lanes, last))

    def own_sweep(l, build, slots):
        base = own_base(l)
        sweep(
            l, own_n[l], own_at[l], 0, base, lambda: feat[pl.ds(base, own_n[l]), :], build, slots, False
        )

    order = list(range(per))[::-1]
    for l in order[:2]:
        own_sweep(l, True, [0])
    pl.semaphore_wait(barrier, F + 1)
    for copy in fr_copies:
        copy.start()
    halo.start()
    for l in order[2:3]:
        own_sweep(l, True, [0])
    for copy in fr_copies:
        copy.wait()
    for k in range(1, F):
        edge_weights(k)
    for l in order[:3]:
        own_sweep(l, False, list(range(1, F)))
    for l in order[3:]:
        own_sweep(l, True, list(range(F)))

    halo.wait()
    for l in range(per):
        if ghost_n[l] == 0:
            raise ValueError(l)
        base = ghost_base(l)
        fill(l, gs[l], ghost_buf[pl.ds(base, ghost_n[l]), width : width + 128], atoms)
        sweep(
            l, ghost_n[l], ghost_at[l], atoms, atoms + side * cap + base,
            lambda l=l, base=base: ghost_buf[pl.ds(base, ghost_n[l]), 0:width], True,
            list(range(F)), True,
        )
    flush()

    for copy in weight_copies:
        copy.wait()
    message = (msg_s[...] * message_scale).astype(BF16)
    hidden = silu(dot(message, w_msg[...])).astype(BF16)
    own = feat[pl.ds(pl.multiple_of(first, 16), nat), :].astype(F32)
    updated = (jnp.concatenate([own] * F, axis=0) + dot(hidden, w_upd[...])).astype(BF16)
    readout = silu(dot(updated, w_read[...])).astype(BF16)
    heads = lax.dot_general(w_heads[...], readout, (((1,), (1,)), ((), ())), preferred_element_type=F32)
    segment = lane1 // nat
    z_s[...] = jnp.zeros_like(z_s)
    for cc in range(3):
        total = jnp.zeros((1, 128), F32)
        for a in range(3):
            rot = jnp.zeros((1, 128), F32)
            for fr in range(F):
                rot = jnp.where(segment == fr, fr_s[fr, a : a + 1, cc : cc + 1], rot)
            total = total + rot * heads[a : a + 1, :]
        z_s[cc : cc + 1, :] = total
    z_s[3:4, :] = heads[3:4, :]
    z = z_s[...]
    total = z
    for k in range(1, F):
        total = total + pltpu.roll(z, k * nat, 1)
    fin_stage[...] = jnp.where(segment == f, total / F, 0.0)
    fin_copies = [
        pltpu.make_async_remote_copy(
            src_ref=fin_stage, dst_ref=fin_s.at[k], send_sem=fin_send.at[k], recv_sem=fin_recv.at[k],
            device_id={"frame": peer}, device_id_type=MESH,
        )
        for k, peer in enumerate(peers)
    ]
    for copy in fin_copies:
        copy.start()
    result = fin_stage[...]
    for k, copy in enumerate(fin_copies):
        copy.wait()
        result = result + fin_s[k]
    out[...] = result[0:4, :]


def local(F, D, features, positions, neighbours, counts, send_rows, frames, w_edge, b_edge,
          w_message, w_update, w_readout, w_heads):
    atoms, width = features.shape
    cap = send_rows.shape[2]
    slots = neighbours.shape[1]
    per = atoms // block_atoms // F
    rows = block_atoms * sum(sum(sizes) for sizes in chunk_sizes(F, atoms, cap))
    vmem = pl.BlockSpec(memory_space=pltpu.VMEM)
    hbm = pl.BlockSpec(memory_space=pltpu.HBM)
    dma = pltpu.SemaphoreType.DMA
    return pl.pallas_call(
        functools.partial(kernel, F, D, atoms, cap, width),
        out_shape=jax.ShapeDtypeStruct((4, atoms), F32),
        in_specs=[hbm] * 12,
        out_specs=vmem,
        scratch_shapes=[
            pltpu.VMEM((atoms, width), BF16),
            pltpu.VMEM((3, atoms), BF16),
            pltpu.VMEM((atoms, slots), jnp.int32),
            pltpu.VMEM((1, atoms), jnp.int32),
            pltpu.VMEM((2, cap), jnp.int32),
            pltpu.VMEM((3, 1, 3), F32),
            pltpu.VMEM((w_edge.shape[0], width), F32),
            pltpu.VMEM((1, width), F32),
            pltpu.VMEM((4, width), BF16),
            pltpu.VMEM((rows, 256), BF16),
            pltpu.VMEM((rows, width), BF16),
            pltpu.VMEM((128, atoms), F32),
            pltpu.VMEM((atoms, slots), F32),
            pltpu.VMEM((atoms, 128), F32),
            pltpu.VMEM((atoms, 128), BF16),
            pltpu.VMEM((cap, width + 128), BF16),
            pltpu.VMEM((cap, width + 128), BF16),
            pltpu.VMEM((per * (atoms + cap), 256), BF16),
            pltpu.VMEM((8, 128), F32),
            pltpu.VMEM((F, 8, 128), F32),
            pltpu.VMEM((32, width), F32),
            pltpu.VMEM((256, F * width), BF16),
            pltpu.VMEM((F * per * block_atoms, width), F32),
            pltpu.VMEM((F * per * block_atoms * 8, width), F32),
            pltpu.VMEM((8, 128), F32),
            pltpu.VMEM((8, 128), F32),
            pltpu.VMEM((F, 8, 128), F32),
            pltpu.VMEM((width, width), BF16),
            pltpu.VMEM((width, width), BF16),
            pltpu.VMEM((width, width), BF16),
            dma((12,)),
            dma,
            dma,
            dma((F - 1,)),
            dma((F - 1,)),
            dma((F - 1,)),
            dma((F - 1,)),
        ],
        compiler_params=pltpu.CompilerParams(
            collective_id=0, has_side_effects=True, vmem_limit_bytes=63 * 1024 * 1024
        ),
    )(
        features, positions, neighbours, counts.reshape(1, -1), send_rows.reshape(2, cap),
        frames.transpose(1, 0, 2), w_edge, b_edge.reshape(1, -1), w_message, w_update, w_readout,
        w_heads.T,
    )


def solution(mesh):
    placed = (
        P("dom", None),
        P(None, "dom"),
        P("dom", None),
        P("dom"),
        P("dom", None, None),
        P("frame", None, None),
        P(),
        P(),
        P(),
        P(),
        P(),
        P(),
    )
    body = functools.partial(local, mesh.shape["frame"], mesh.shape["dom"])
    return jax.shard_map(
        body, mesh=mesh, in_specs=placed, out_specs=P(None, "dom"), check_vma=False
    )
```

```python
import functools

import jax
import jax.numpy as jnp
from jax import lax
from jax.experimental import pallas as pl
from jax.experimental.pallas import tpu as pltpu
from jax.sharding import PartitionSpec as P

F32 = jnp.float32
BF16 = jnp.bfloat16
MESH = pl.DeviceIdType.MESH
WINDOW = 128
message_scale = 0.0884
radial_step = 1.25
block_atoms = 16
ROWS = 512
COLS = 512


def iota(shape, dim):
    return lax.broadcasted_iota(jnp.int32, shape, dim)


def dot(a, b):
    return jnp.dot(a, b, preferred_element_type=F32)


def split(value):
    high = value.astype(BF16).astype(F32)
    return high, value - high


def silu(x):
    half = 0.5 * x
    return half + half * jnp.tanh(half)


def up16(n):
    return (n + 15) // 16 * 16


def chunk_sizes(F, atoms, cap):
    blocks = atoms // block_atoms
    per = blocks // F
    span = atoms + 2 * cap - WINDOW
    own, ghost = [0] * per, [0] * per
    for f in range(F):
        for b in range(f * per, (f + 1) * per):
            start = b * span // max(blocks - 1, 1)
            low, high = max(start - cap, 0), min(start + WINDOW - cap, atoms)
            below, above = max(cap - start, 0), max(start + WINDOW - cap - atoms, 0)
            if f < F // 2:
                assert above == 0
                l, need, gh = b - f * per, high, below
            else:
                assert below == 0
                l, need, gh = (f + 1) * per - 1 - b, atoms - low, above
            own[l] = max(own[l], up16(need))
            ghost[l] = max(ghost[l], up16(gh))
    return own, ghost


def kernel(
    F, D, atoms, cap, width,
    feat_h, pos_h, nbr_h, cnt_h, send_h, frames_h, w_edge_h, b_edge_h, w_msg_h, w_upd_h, w_read_h,
    w_heads_h,
    out,
    feat, pos, nbr, cnt, send, frames, w_edge, b_edge, w_heads,
    left_s, wgt_s, table, nbr_s, add_s, own_u, send_buf, ghost_buf, lhs, fr_stage, fr_s, base_s, wst,
    msg_s, acc_s, z_s, fin_stage, fin_s, w_msg, w_upd, w_read,
    w_sem, halo_send, halo_recv, fr_send, fr_recv, fin_send, fin_recv,
):
    f = lax.axis_index("frame")
    d = lax.axis_index("dom")
    side = f // (F // 2)
    blocks = atoms // block_atoms
    per = blocks // F
    nat = per * block_atoms
    own_n, ghost_n = chunk_sizes(F, atoms, cap)
    region = atoms + cap
    first = f * nat

    barrier = pltpu.get_barrier_semaphore()
    peers = [lax.rem(f + k, F) for k in range(1, F)]
    up, down = lax.rem(d + 1, D), lax.rem(d + D - 1, D)
    for peer in peers:
        pl.semaphore_signal(barrier, inc=1, device_id={"frame": peer}, device_id_type=MESH)
    for near in (up, down):
        pl.semaphore_signal(barrier, inc=1, device_id={"dom": near}, device_id_type=MESH)
    moves = (
        (pos_h, pos), (cnt_h, cnt), (send_h, send), (feat_h, feat), (frames_h, frames),
        (nbr_h, nbr), (w_edge_h, w_edge), (b_edge_h, b_edge),
        (w_msg_h, w_msg), (w_upd_h, w_upd), (w_read_h, w_read), (w_heads_h, w_heads),
    )
    copies = [pltpu.make_async_copy(src, dst, w_sem.at[n]) for n, (src, dst) in enumerate(moves)]
    for copy in copies:
        copy.start()
    weight_copies = copies[8:]

    lane = iota((128, 128), 1)
    row = iota((128, 128), 0)
    lane1 = iota((1, 128), 1)
    group = lane1 >> 3
    radial = lane1 & 7
    special1 = radial >= 6

    copies[0].wait()
    copies[1].wait()
    table[...] = jnp.zeros_like(table)
    table[0:3, :] = pos[...].astype(F32)
    table[3:4, :] = cnt[...].astype(F32)
    by_atom = table[...].T
    sq = jnp.sum(jnp.where(lane < 3, by_atom * by_atom, 0.0), axis=1, keepdims=True)
    sq_hi, rest = split(sq)
    sq_mid, sq_lo = split(rest)
    u = jnp.where(lane < 3, by_atom, 0.0)
    u = jnp.where(lane == 3, sq_hi, u)
    u = jnp.where(lane == 4, sq_mid, u)
    u = jnp.where(lane == 5, sq_lo, u)
    u = jnp.where((lane >= 6) & (lane < 9), 1.0, u)
    own_u[...] = u.astype(BF16)

    copies[4].wait()
    fr_stage[...] = jnp.zeros_like(fr_stage)
    for a in range(3):
        fr_stage[a : a + 1, 0:3] = frames[a]
    fr_s[0] = fr_stage[...]
    copies[2].wait()
    copies[3].wait()
    chosen = jnp.where(side == 0, send[1:2, :], send[0:1, :])
    pick = (iota((atoms, cap), 0) == chosen).astype(F32).T.astype(BF16)
    send_buf[:, 0:width] = dot(pick, feat[...]).astype(BF16)
    send_buf[:, width : width + 128] = dot(pick, own_u[...]).astype(BF16)
    halo = pltpu.make_async_remote_copy(
        src_ref=send_buf, dst_ref=ghost_buf, send_sem=halo_send, recv_sem=halo_recv,
        device_id={"dom": jnp.where(side == 0, up, down)}, device_id_type=MESH,
    )
    fr_copies = [
        pltpu.make_async_remote_copy(
            src_ref=fr_stage, dst_ref=fr_s.at[F - k], send_sem=fr_send.at[k - 1],
            recv_sem=fr_recv.at[F - k - 1], device_id={"frame": peers[k - 1]}, device_id_type=MESH,
        )
        for k in range(1, F)
    ]

    copies[5].wait()
    live = iota((atoms, nbr.shape[1]), 1).astype(F32) < by_atom[:, 3:4]
    nbr_s[...] = jnp.where(live, nbr[...].astype(F32), -1.0)

    spot = jnp.where(special1, group * 2 + radial - 6, -1)
    place_row = jnp.where(spot < 3, spot, jnp.where(spot < 6, spot - 3, -1))
    neg_row = jnp.where((spot >= 6) & (spot < 9), spot - 6, -1)
    neg_row = jnp.where((spot >= 9) & (spot < 12), spot - 9, neg_row)
    one_row = jnp.where((spot >= 12) & (spot < 14), 6, -1)
    place_add = jnp.where(row == one_row, 1.0, jnp.where(row == neg_row, -1.0, 0.0)).astype(BF16)
    add_s[...] = dot(own_u[...], place_add)
    place = jnp.where(row == place_row, 1.0, 0.0).astype(BF16)
    centres = radial.astype(F32) * radial_step

    def block_rows(l):
        return (l * (1 - side) + (per - 1 - l) * side) * block_atoms

    def own_base(l):
        return pl.multiple_of(side * (atoms - own_n[l]), 16)

    def ghost_base(l):
        return pl.multiple_of((1 - side) * (cap - ghost_n[l]), 16)

    def geometry(l):
        start = first + block_rows(l)
        expand = jnp.where(row == start + group, 1.0, 0.0).astype(BF16)
        centre = dot(table[0:16, :].astype(BF16), expand)
        sub = iota((16, 128), 0)
        sqi = jnp.sum(jnp.where(sub < 3, centre * centre, 0.0), axis=0, keepdims=True) + 0.25
        hi, tail = split(sqi)
        mid, lo = split(tail)
        g = jnp.where(sub < 3, -2.0 * centre, jnp.where(sub < 6, 1.0, 0.0))
        for c, part in enumerate((hi, mid, lo)):
            g = jnp.where(sub == 6 + c, part, g)
        g = jnp.concatenate([g.astype(BF16), jnp.zeros((112, 128), BF16)], axis=0)
        return jnp.concatenate([g, place], axis=1)

    def fill(l, g, rows_u, offset):
        n = rows_u.shape[0]
        both = dot(rows_u, g)
        d2, placed = both[:, 0:128], both[:, 128:256]
        dist = jnp.sqrt(jnp.maximum(d2, 0.25))
        gap = dist - centres
        value = jnp.exp(-(gap * gap))
        at = l * region + offset
        lhs[at : at + n, 0:128] = jnp.where(special1, 0.0, value).astype(BF16)
        lhs[at : at + n, 128:256] = jnp.where(special1, placed, value).astype(BF16)

    gs = []
    for l in range(per):
        g = geometry(l)
        gs.append(g)
        fill(l, g, own_u[pl.ds(own_base(l), own_n[l]), :], 0)

    def wanted(second):
        want = jnp.where(special1, -1, radial + 6 * second)
        if second:
            want = jnp.where((spot >= 0) & (spot < 6), spot + 12, want)
            want = jnp.where((spot >= 6) & (spot < 14), spot + 6, want)
        return jnp.where(iota((32, 128), 0) == want, 1.0, 0.0).T.astype(BF16)

    sel = jnp.concatenate([wanted(0), wanted(1)], axis=0)
    copies[6].wait()
    copies[7].wait()
    base_s[...] = jnp.zeros_like(base_s)
    hi, lo = split(0.5 * w_edge[0:6, :])
    base_s[0:6, :] = hi
    base_s[6:12, :] = lo
    hi, lo = split(0.5 * b_edge[...])
    base_s[18:19, :] = hi
    base_s[19:20, :] = lo

    def edge_weights(fr):
        for cc in range(3):
            acc = fr_s[fr, 0:1, cc : cc + 1] * w_edge[6:7, :]
            acc = acc + fr_s[fr, 1:2, cc : cc + 1] * w_edge[7:8, :]
            acc = acc + fr_s[fr, 2:3, cc : cc + 1] * w_edge[8:9, :]
            hi, lo = split(0.5 * acc)
            base_s[12 + cc : 13 + cc, :] = hi
            base_s[15 + cc : 16 + cc, :] = lo
        wst[:, fr * width : (fr + 1) * width] = dot(sel, base_s[...].astype(BF16)).astype(BF16)

    edge_weights(0)

    own_at = [block_atoms * sum(own_n[:l]) for l in range(per)]
    ghost_at = [block_atoms * (sum(own_n) + sum(ghost_n[:l])) for l in range(per)]

    pending = []

    def flush():
        while pending:
            pending.pop()()

    def finish(h, at, n, atoms_here, fr, lanes, last):
        terms = (h + h * jnp.tanh(h)) * wgt_s[at : at + len(atoms_here) * n, lanes : lanes + COLS]
        for j, local in enumerate(atoms_here):
            parts = [terms[j * n + r : j * n + r + 16, :] for r in range(0, n, 16)]
            while len(parts) > 1:
                parts = [sum(parts[r + 1 : r + 2], parts[r]) for r in range(0, len(parts), 2)]
            total = parts[0].astype(F32)
            total = total[0:8, :] + total[8:16, :]
            eight = pl.ds(pl.multiple_of((fr * nat + local) * 8, 8), 8)
            if last:
                total = total + acc_s[eight, lanes : lanes + COLS]
                spot = pl.ds(fr * nat + local, 1)
                msg_s[spot, lanes : lanes + COLS] = jnp.sum(total, axis=0, keepdims=True)
            else:
                acc_s[eight, lanes : lanes + COLS] = total

    def sweep(l, n, at, offset, first_id, load_feat, build, slots, last):
        many = max(k for k in (1, 2, 4, 8, 16) if k * n <= ROWS)
        ids = (first_id + iota((n, 128), 0)).astype(F32)
        for k in range(0, block_atoms, many):
            here = at + k * n
            for i in range(k, k + many if build else k):
                rows = slice(at + i * n, at + i * n + n)
                own_row = pl.ds(first + block_rows(l) + i, 1)
                mult = jnp.sum(jnp.where(ids == nbr_s[own_row, :], 1.0, 0.0), axis=1, keepdims=True)
                wgt_s[rows, :] = load_feat() * mult.astype(BF16)
                mask = jnp.where((group == i) & (~special1), 1.0, 0.0)
                left1 = lhs[l * region + offset : l * region + offset + n, 0:128] * mask.astype(BF16)
                left2 = lhs[l * region + offset : l * region + offset + n, 128:256]
                left2 = left2 * jnp.where(special1, 1.0, mask).astype(BF16) + add_s[own_row, :].astype(BF16)
                left_s[rows, 0:128] = left1
                left_s[rows, 128:256] = left2
            atoms_here = [block_rows(l) + i for i in range(k, k + many)]
            for fr in slots:
                for lanes in range(0, width, COLS):
                    c = fr * width + lanes
                    h = dot(left_s[here : here + many * n, :], wst[:, c : c + COLS]).astype(BF16)
                    flush()
                    pending.append(functools.partial(finish, h, here, n, atoms_here, fr, lanes, last))

    def own_sweep(l, build, slots):
        base = own_base(l)
        sweep(
            l, own_n[l], own_at[l], 0, base, lambda: feat[pl.ds(base, own_n[l]), :], build, slots, False
        )

    order = list(range(per))[::-1]
    for l in order[:2]:
        own_sweep(l, True, [0])
    pl.semaphore_wait(barrier, F + 1)
    for copy in fr_copies:
        copy.start()
    halo.start()
    for l in order[2:3]:
        own_sweep(l, True, [0])
    for copy in fr_copies:
        copy.wait()
    for k in range(1, F):
        edge_weights(k)
    for l in order[:3]:
        own_sweep(l, False, list(range(1, F)))
    for l in order[3:]:
        own_sweep(l, True, list(range(F)))

    halo.wait()
    for l in range(per):
        if ghost_n[l] == 0:
            raise ValueError(l)
        base = ghost_base(l)
        fill(l, gs[l], ghost_buf[pl.ds(base, ghost_n[l]), width : width + 128], atoms)
        sweep(
            l, ghost_n[l], ghost_at[l], atoms, atoms + side * cap + base,
            lambda l=l, base=base: ghost_buf[pl.ds(base, ghost_n[l]), 0:width], True,
            list(range(F)), True,
        )
    flush()

    for copy in weight_copies:
        copy.wait()
    message = (msg_s[...] * message_scale).astype(BF16)
    hidden = silu(dot(message, w_msg[...])).astype(BF16)
    own = feat[pl.ds(pl.multiple_of(first, 16), nat), :].astype(F32)
    updated = (jnp.concatenate([own] * F, axis=0) + dot(hidden, w_upd[...])).astype(BF16)
    readout = silu(dot(updated, w_read[...])).astype(BF16)
    heads = lax.dot_general(w_heads[...], readout, (((1,), (1,)), ((), ())), preferred_element_type=F32)
    segment = lane1 // nat
    z_s[...] = jnp.zeros_like(z_s)
    for cc in range(3):
        total = jnp.zeros((1, 128), F32)
        for a in range(3):
            rot = jnp.zeros((1, 128), F32)
            for fr in range(F):
                rot = jnp.where(segment == fr, fr_s[fr, a : a + 1, cc : cc + 1], rot)
            total = total + rot * heads[a : a + 1, :]
        z_s[cc : cc + 1, :] = total
    z_s[3:4, :] = heads[3:4, :]
    z = z_s[...]
    total = z
    for k in range(1, F):
        total = total + pltpu.roll(z, k * nat, 1)
    fin_stage[...] = jnp.where(segment == f, total / F, 0.0)
    fin_copies = [
        pltpu.make_async_remote_copy(
            src_ref=fin_stage, dst_ref=fin_s.at[k], send_sem=fin_send.at[k], recv_sem=fin_recv.at[k],
            device_id={"frame": peer}, device_id_type=MESH,
        )
        for k, peer in enumerate(peers)
    ]
    for copy in fin_copies:
        copy.start()
    result = fin_stage[...]
    for k, copy in enumerate(fin_copies):
        copy.wait()
        result = result + fin_s[k]
    out[...] = result[0:4, :]


def local(F, D, features, positions, neighbours, counts, send_rows, frames, w_edge, b_edge,
          w_message, w_update, w_readout, w_heads):
    atoms, width = features.shape
    cap = send_rows.shape[2]
    slots = neighbours.shape[1]
    per = atoms // block_atoms // F
    rows = block_atoms * sum(sum(sizes) for sizes in chunk_sizes(F, atoms, cap))
    vmem = pl.BlockSpec(memory_space=pltpu.VMEM)
    hbm = pl.BlockSpec(memory_space=pltpu.HBM)
    dma = pltpu.SemaphoreType.DMA
    return pl.pallas_call(
        functools.partial(kernel, F, D, atoms, cap, width),
        out_shape=jax.ShapeDtypeStruct((4, atoms), F32),
        in_specs=[hbm] * 12,
        out_specs=vmem,
        scratch_shapes=[
            pltpu.VMEM((atoms, width), BF16),
            pltpu.VMEM((3, atoms), BF16),
            pltpu.VMEM((atoms, slots), jnp.int32),
            pltpu.VMEM((1, atoms), jnp.int32),
            pltpu.VMEM((2, cap), jnp.int32),
            pltpu.VMEM((3, 1, 3), F32),
            pltpu.VMEM((w_edge.shape[0], width), F32),
            pltpu.VMEM((1, width), F32),
            pltpu.VMEM((4, width), BF16),
            pltpu.VMEM((rows, 256), BF16),
            pltpu.VMEM((rows, width), BF16),
            pltpu.VMEM((128, atoms), F32),
            pltpu.VMEM((atoms, slots), F32),
            pltpu.VMEM((atoms, 128), F32),
            pltpu.VMEM((atoms, 128), BF16),
            pltpu.VMEM((cap, width + 128), BF16),
            pltpu.VMEM((cap, width + 128), BF16),
            pltpu.VMEM((per * (atoms + cap), 256), BF16),
            pltpu.VMEM((8, 128), F32),
            pltpu.VMEM((F, 8, 128), F32),
            pltpu.VMEM((32, width), F32),
            pltpu.VMEM((256, F * width), BF16),
            pltpu.VMEM((F * per * block_atoms, width), F32),
            pltpu.VMEM((F * per * block_atoms * 8, width), F32),
            pltpu.VMEM((8, 128), F32),
            pltpu.VMEM((8, 128), F32),
            pltpu.VMEM((F, 8, 128), F32),
            pltpu.VMEM((width, width), BF16),
            pltpu.VMEM((width, width), BF16),
            pltpu.VMEM((width, width), BF16),
            dma((12,)),
            dma,
            dma,
            dma((F - 1,)),
            dma((F - 1,)),
            dma((F - 1,)),
            dma((F - 1,)),
        ],
        compiler_params=pltpu.CompilerParams(
            collective_id=0, has_side_effects=True, vmem_limit_bytes=63 * 1024 * 1024
        ),
    )(
        features, positions, neighbours, counts.reshape(1, -1), send_rows.reshape(2, cap),
        frames.transpose(1, 0, 2), w_edge, b_edge.reshape(1, -1), w_message, w_update, w_readout,
        w_heads.T,
    )


def solution(mesh):
    placed = (
        P("dom", None),
        P(None, "dom"),
        P("dom", None),
        P("dom"),
        P("dom", None, None),
        P("frame", None, None),
        P(),
        P(),
        P(),
        P(),
        P(),
        P(),
    )
    body = functools.partial(local, mesh.shape["frame"], mesh.shape["dom"])
    return jax.shard_map(
        body, mesh=mesh, in_specs=placed, out_specs=P(None, "dom"), check_vma=False
    )
```

```python
import functools

import jax
import jax.numpy as jnp
from jax import lax
from jax.experimental import pallas as pl
from jax.experimental.pallas import tpu as pltpu
from jax.sharding import PartitionSpec as P

F32 = jnp.float32
BF16 = jnp.bfloat16
MESH = pl.DeviceIdType.MESH
WINDOW = 128
message_scale = 0.0884
radial_step = 1.25
block_atoms = 16
ROWS = 512
COLS = 512
HALF = 8


def iota(shape, dim):
    return lax.broadcasted_iota(jnp.int32, shape, dim)


def dot(a, b):
    return jnp.dot(a, b, preferred_element_type=F32)


def split(value):
    high = value.astype(BF16).astype(F32)
    return high, value - high


def silu(x):
    half = 0.5 * x
    return half + half * jnp.tanh(half)


def up16(n):
    return (n + 15) // 16 * 16


def chunk_sizes(F, atoms, cap):
    blocks = atoms // block_atoms
    per = blocks // F
    span = atoms + 2 * cap - WINDOW
    own, ghost = [0] * per, [0] * per
    for f in range(F):
        for b in range(f * per, (f + 1) * per):
            start = b * span // max(blocks - 1, 1)
            low, high = max(start - cap, 0), min(start + WINDOW - cap, atoms)
            below, above = max(cap - start, 0), max(start + WINDOW - cap - atoms, 0)
            if f < F // 2:
                assert above == 0
                l, need, gh = b - f * per, high, below
            else:
                assert below == 0
                l, need, gh = (f + 1) * per - 1 - b, atoms - low, above
            own[l] = max(own[l], up16(need))
            ghost[l] = max(ghost[l], up16(gh))
    return own, ghost


def kernel(
    F, D, atoms, cap, width,
    feat_h, pos_h, nbr_h, cnt_h, send_h, frames_h, w_edge_h, b_edge_h, w_msg_h, w_upd_h, w_read_h,
    w_heads_h,
    out,
    feat, pos, nbr, cnt, send, frames, w_edge, b_edge, w_heads,
    left_s, wgt_s, table, nbr_s, add_s, own_u, send_buf, ghost_buf, lhs, fr_stage, fr_s, base_s, wst,
    msg_s, acc_s, z_s, fin_stage, fin_s, w_msg, w_upd, w_read,
    w_sem, halo_send, halo_recv, fr_send, fr_recv, fin_send, fin_recv,
):
    f = lax.axis_index("frame")
    d = lax.axis_index("dom")
    side = f // (F // 2)
    blocks = atoms // block_atoms
    per = blocks // F
    nat = per * block_atoms
    own_n, ghost_n = chunk_sizes(F, atoms, cap)
    region = atoms + cap
    first = f * nat

    barrier = pltpu.get_barrier_semaphore()
    peers = [lax.rem(f + k, F) for k in range(1, F)]
    up, down = lax.rem(d + 1, D), lax.rem(d + D - 1, D)
    for peer in peers:
        pl.semaphore_signal(barrier, inc=1, device_id={"frame": peer}, device_id_type=MESH)
    for near in (up, down):
        pl.semaphore_signal(barrier, inc=1, device_id={"dom": near}, device_id_type=MESH)
    moves = (
        (pos_h, pos), (cnt_h, cnt), (send_h, send), (feat_h, feat), (frames_h, frames),
        (nbr_h, nbr), (w_edge_h, w_edge), (b_edge_h, b_edge),
        (w_msg_h, w_msg), (w_upd_h, w_upd), (w_read_h, w_read), (w_heads_h, w_heads),
    )
    copies = [pltpu.make_async_copy(src, dst, w_sem.at[n]) for n, (src, dst) in enumerate(moves)]
    for copy in copies:
        copy.start()
    weight_copies = copies[8:]

    lane = iota((128, 128), 1)
    row = iota((128, 128), 0)
    lane1 = iota((1, 128), 1)
    group = lane1 >> 3
    radial = lane1 & 7
    special1 = radial >= 6

    copies[0].wait()
    copies[1].wait()
    table[...] = jnp.zeros_like(table)
    table[0:3, :] = pos[...].astype(F32)
    table[3:4, :] = cnt[...].astype(F32)
    by_atom = table[...].T
    sq = jnp.sum(jnp.where(lane < 3, by_atom * by_atom, 0.0), axis=1, keepdims=True)
    sq_hi, rest = split(sq)
    sq_mid, sq_lo = split(rest)
    u = jnp.where(lane < 3, by_atom, 0.0)
    u = jnp.where(lane == 3, sq_hi, u)
    u = jnp.where(lane == 4, sq_mid, u)
    u = jnp.where(lane == 5, sq_lo, u)
    u = jnp.where((lane >= 6) & (lane < 9), 1.0, u)
    own_u[...] = u.astype(BF16)

    copies[4].wait()
    fr_stage[...] = jnp.zeros_like(fr_stage)
    for a in range(3):
        fr_stage[a : a + 1, 0:3] = frames[a]
    fr_s[0] = fr_stage[...]
    copies[2].wait()
    copies[3].wait()
    chosen = jnp.where(side == 0, send[1:2, :], send[0:1, :])
    pick = (iota((atoms, cap), 0) == chosen).astype(F32).T.astype(BF16)
    send_buf[:, 0:width] = dot(pick, feat[...]).astype(BF16)
    send_buf[:, width : width + 128] = dot(pick, own_u[...]).astype(BF16)
    halo = pltpu.make_async_remote_copy(
        src_ref=send_buf, dst_ref=ghost_buf, send_sem=halo_send, recv_sem=halo_recv,
        device_id={"dom": jnp.where(side == 0, up, down)}, device_id_type=MESH,
    )
    fr_copies = [
        pltpu.make_async_remote_copy(
            src_ref=fr_stage, dst_ref=fr_s.at[F - k], send_sem=fr_send.at[k - 1],
            recv_sem=fr_recv.at[F - k - 1], device_id={"frame": peers[k - 1]}, device_id_type=MESH,
        )
        for k in range(1, F)
    ]

    copies[5].wait()
    live = iota((atoms, nbr.shape[1]), 1).astype(F32) < by_atom[:, 3:4]
    nbr_s[...] = jnp.where(live, nbr[...].astype(F32), -1.0)

    spot = jnp.where(special1, group * 2 + radial - 6, -1)
    place_row = jnp.where(spot < 3, spot, jnp.where(spot < 6, spot - 3, -1))
    neg_row = jnp.where((spot >= 6) & (spot < 9), spot - 6, -1)
    neg_row = jnp.where((spot >= 9) & (spot < 12), spot - 9, neg_row)
    one_row = jnp.where((spot >= 12) & (spot < 14), 6, -1)
    place_add = jnp.where(row == one_row, 1.0, jnp.where(row == neg_row, -1.0, 0.0)).astype(BF16)
    add_s[...] = dot(own_u[...], place_add)
    place = jnp.where(row == place_row, 1.0, 0.0).astype(BF16)
    centres = radial.astype(F32) * radial_step

    def block_rows(l):
        return (l * (1 - side) + (per - 1 - l) * side) * block_atoms

    def own_base(l):
        return pl.multiple_of(side * (atoms - own_n[l]), 16)

    def ghost_base(l):
        return pl.multiple_of((1 - side) * (cap - ghost_n[l]), 16)

    def geometry(l):
        start = first + block_rows(l)
        expand = jnp.where(row == start + group, 1.0, 0.0).astype(BF16)
        centre = dot(table[0:16, :].astype(BF16), expand)
        sub = iota((16, 128), 0)
        sqi = jnp.sum(jnp.where(sub < 3, centre * centre, 0.0), axis=0, keepdims=True) + 0.25
        hi, tail = split(sqi)
        mid, lo = split(tail)
        g = jnp.where(sub < 3, -2.0 * centre, jnp.where(sub < 6, 1.0, 0.0))
        for c, part in enumerate((hi, mid, lo)):
            g = jnp.where(sub == 6 + c, part, g)
        g = jnp.concatenate([g.astype(BF16), jnp.zeros((112, 128), BF16)], axis=0)
        return jnp.concatenate([g, place], axis=1)

    def fill(l, g, rows_u, offset):
        n = rows_u.shape[0]
        both = dot(rows_u, g)
        d2, placed = both[:, 0:128], both[:, 128:256]
        dist = jnp.sqrt(jnp.maximum(d2, 0.25))
        gap = dist - centres
        value = jnp.exp(-(gap * gap))
        at = l * region + offset
        lhs[at : at + n, 0:128] = jnp.where(special1, 0.0, value).astype(BF16)
        lhs[at : at + n, 128:256] = jnp.where(special1, placed, value).astype(BF16)

    gs = []
    for l in range(per):
        g = geometry(l)
        gs.append(g)
        fill(l, g, own_u[pl.ds(own_base(l), own_n[l]), :], 0)

    def wanted(second):
        want = jnp.where(special1, -1, radial + 6 * second)
        if second:
            want = jnp.where((spot >= 0) & (spot < 6), spot + 12, want)
            want = jnp.where((spot >= 6) & (spot < 14), spot + 6, want)
        return jnp.where(iota((32, 128), 0) == want, 1.0, 0.0).T.astype(BF16)

    sel = jnp.concatenate([wanted(0), wanted(1)], axis=0)
    copies[6].wait()
    copies[7].wait()
    base_s[...] = jnp.zeros_like(base_s)
    hi, lo = split(0.5 * w_edge[0:6, :])
    base_s[0:6, :] = hi
    base_s[6:12, :] = lo
    hi, lo = split(0.5 * b_edge[...])
    base_s[18:19, :] = hi
    base_s[19:20, :] = lo

    def edge_weights(fr):
        for cc in range(3):
            acc = fr_s[fr, 0:1, cc : cc + 1] * w_edge[6:7, :]
            acc = acc + fr_s[fr, 1:2, cc : cc + 1] * w_edge[7:8, :]
            acc = acc + fr_s[fr, 2:3, cc : cc + 1] * w_edge[8:9, :]
            hi, lo = split(0.5 * acc)
            base_s[12 + cc : 13 + cc, :] = hi
            base_s[15 + cc : 16 + cc, :] = lo
        wst[:, fr * width : (fr + 1) * width] = dot(sel, base_s[...].astype(BF16)).astype(BF16)

    edge_weights(0)

    own_at = [block_atoms * sum(own_n[:l]) for l in range(per)]
    ghost_at = [block_atoms * (sum(own_n) + sum(ghost_n[:l])) for l in range(per)]

    pending = []

    def flush():
        while pending:
            pending.pop()()

    def finish(h, at, n, atoms_here, fr, lanes, last):
        terms = (h + h * jnp.tanh(h)) * wgt_s[pl.ds(at, len(atoms_here) * n), lanes : lanes + COLS]
        for j, local in enumerate(atoms_here):
            parts = [terms[j * n + r : j * n + r + 16, :] for r in range(0, n, 16)]
            while len(parts) > 1:
                parts = [sum(parts[r + 1 : r + 2], parts[r]) for r in range(0, len(parts), 2)]
            total = parts[0].astype(F32)
            total = total[0:8, :] + total[8:16, :]
            eight = pl.ds(pl.multiple_of((fr * nat + local) * 8, 8), 8)
            if last:
                total = total + acc_s[eight, lanes : lanes + COLS]
                spot = pl.ds(fr * nat + local, 1)
                msg_s[spot, lanes : lanes + COLS] = jnp.sum(total, axis=0, keepdims=True)
            else:
                acc_s[eight, lanes : lanes + COLS] = total

    def sweep(l, n, at, offset, first_id, load_feat, build, slots, last):
        many = max(k for k in (1, 2, 4, 8, 16) if k * n <= ROWS)
        ids = (first_id + iota((n, 128), 0)).astype(F32)
        many = min(many, HALF)

        def step(half, _):
            for k in range(0, HALF, many):
                here = pl.multiple_of(at + (half * HALF + k) * n, 16)
                for j in range(many if build else 0):
                    i = half * HALF + k + j
                    rows = pl.ds(pl.multiple_of(here + j * n, 16), n)
                    own_row = pl.ds(first + block_rows(l) + i, 1)
                    mult = jnp.sum(jnp.where(ids == nbr_s[own_row, :], 1.0, 0.0), axis=1, keepdims=True)
                    wgt_s[rows, :] = load_feat() * mult.astype(BF16)
                    mask = jnp.where((group == i) & (~special1), 1.0, 0.0)
                    left1 = lhs[l * region + offset : l * region + offset + n, 0:128] * mask.astype(BF16)
                    left2 = lhs[l * region + offset : l * region + offset + n, 128:256]
                    left2 = left2 * jnp.where(special1, 1.0, mask).astype(BF16) + add_s[own_row, :].astype(BF16)
                    left_s[rows, 0:128] = left1
                    left_s[rows, 128:256] = left2
                atoms_here = [block_rows(l) + half * HALF + k + j for j in range(many)]
                for fr in slots:
                    for lanes in range(0, width, COLS):
                        c = fr * width + lanes
                        h = dot(left_s[pl.ds(here, many * n), :], wst[:, c : c + COLS]).astype(BF16)
                        flush()
                        pending.append(functools.partial(finish, h, here, n, atoms_here, fr, lanes, last))
            flush()
            return 0

        flush()
        lax.fori_loop(0, block_atoms // HALF, step, 0)

    def own_sweep(l, build, slots):
        base = own_base(l)
        sweep(
            l, own_n[l], own_at[l], 0, base, lambda: feat[pl.ds(base, own_n[l]), :], build, slots, False
        )

    order = list(range(per))[::-1]
    for l in order[:2]:
        own_sweep(l, True, [0])
    pl.semaphore_wait(barrier, F + 1)
    for copy in fr_copies:
        copy.start()
    halo.start()
    for l in order[2:3]:
        own_sweep(l, True, [0])
    for copy in fr_copies:
        copy.wait()
    for k in range(1, F):
        edge_weights(k)
    for l in order[:3]:
        own_sweep(l, False, list(range(1, F)))
    for l in order[3:]:
        own_sweep(l, True, list(range(F)))

    halo.wait()
    for l in range(per):
        if ghost_n[l] == 0:
            raise ValueError(l)
        base = ghost_base(l)
        fill(l, gs[l], ghost_buf[pl.ds(base, ghost_n[l]), width : width + 128], atoms)
        sweep(
            l, ghost_n[l], ghost_at[l], atoms, atoms + side * cap + base,
            lambda l=l, base=base: ghost_buf[pl.ds(base, ghost_n[l]), 0:width], True,
            list(range(F)), True,
        )
    flush()

    for copy in weight_copies:
        copy.wait()
    message = (msg_s[...] * message_scale).astype(BF16)
    hidden = silu(dot(message, w_msg[...])).astype(BF16)
    own = feat[pl.ds(pl.multiple_of(first, 16), nat), :].astype(F32)
    updated = (jnp.concatenate([own] * F, axis=0) + dot(hidden, w_upd[...])).astype(BF16)
    readout = silu(dot(updated, w_read[...])).astype(BF16)
    heads = lax.dot_general(w_heads[...], readout, (((1,), (1,)), ((), ())), preferred_element_type=F32)
    segment = lane1 // nat
    z_s[...] = jnp.zeros_like(z_s)
    for cc in range(3):
        total = jnp.zeros((1, 128), F32)
        for a in range(3):
            rot = jnp.zeros((1, 128), F32)
            for fr in range(F):
                rot = jnp.where(segment == fr, fr_s[fr, a : a + 1, cc : cc + 1], rot)
            total = total + rot * heads[a : a + 1, :]
        z_s[cc : cc + 1, :] = total
    z_s[3:4, :] = heads[3:4, :]
    z = z_s[...]
    total = z
    for k in range(1, F):
        total = total + pltpu.roll(z, k * nat, 1)
    fin_stage[...] = jnp.where(segment == f, total / F, 0.0)
    fin_copies = [
        pltpu.make_async_remote_copy(
            src_ref=fin_stage, dst_ref=fin_s.at[k], send_sem=fin_send.at[k], recv_sem=fin_recv.at[k],
            device_id={"frame": peer}, device_id_type=MESH,
        )
        for k, peer in enumerate(peers)
    ]
    for copy in fin_copies:
        copy.start()
    result = fin_stage[...]
    for k, copy in enumerate(fin_copies):
        copy.wait()
        result = result + fin_s[k]
    out[...] = result[0:4, :]


def local(F, D, features, positions, neighbours, counts, send_rows, frames, w_edge, b_edge,
          w_message, w_update, w_readout, w_heads):
    atoms, width = features.shape
    cap = send_rows.shape[2]
    slots = neighbours.shape[1]
    per = atoms // block_atoms // F
    rows = block_atoms * sum(sum(sizes) for sizes in chunk_sizes(F, atoms, cap))
    vmem = pl.BlockSpec(memory_space=pltpu.VMEM)
    hbm = pl.BlockSpec(memory_space=pltpu.HBM)
    dma = pltpu.SemaphoreType.DMA
    return pl.pallas_call(
        functools.partial(kernel, F, D, atoms, cap, width),
        out_shape=jax.ShapeDtypeStruct((4, atoms), F32),
        in_specs=[hbm] * 12,
        out_specs=vmem,
        scratch_shapes=[
            pltpu.VMEM((atoms, width), BF16),
            pltpu.VMEM((3, atoms), BF16),
            pltpu.VMEM((atoms, slots), jnp.int32),
            pltpu.VMEM((1, atoms), jnp.int32),
            pltpu.VMEM((2, cap), jnp.int32),
            pltpu.VMEM((3, 1, 3), F32),
            pltpu.VMEM((w_edge.shape[0], width), F32),
            pltpu.VMEM((1, width), F32),
            pltpu.VMEM((4, width), BF16),
            pltpu.VMEM((rows, 256), BF16),
            pltpu.VMEM((rows, width), BF16),
            pltpu.VMEM((128, atoms), F32),
            pltpu.VMEM((atoms, slots), F32),
            pltpu.VMEM((atoms, 128), F32),
            pltpu.VMEM((atoms, 128), BF16),
            pltpu.VMEM((cap, width + 128), BF16),
            pltpu.VMEM((cap, width + 128), BF16),
            pltpu.VMEM((per * (atoms + cap), 256), BF16),
            pltpu.VMEM((8, 128), F32),
            pltpu.VMEM((F, 8, 128), F32),
            pltpu.VMEM((32, width), F32),
            pltpu.VMEM((256, F * width), BF16),
            pltpu.VMEM((F * per * block_atoms, width), F32),
            pltpu.VMEM((F * per * block_atoms * 8, width), F32),
            pltpu.VMEM((8, 128), F32),
            pltpu.VMEM((8, 128), F32),
            pltpu.VMEM((F, 8, 128), F32),
            pltpu.VMEM((width, width), BF16),
            pltpu.VMEM((width, width), BF16),
            pltpu.VMEM((width, width), BF16),
            dma((12,)),
            dma,
            dma,
            dma((F - 1,)),
            dma((F - 1,)),
            dma((F - 1,)),
            dma((F - 1,)),
        ],
        compiler_params=pltpu.CompilerParams(
            collective_id=0, has_side_effects=True, vmem_limit_bytes=63 * 1024 * 1024
        ),
    )(
        features, positions, neighbours, counts.reshape(1, -1), send_rows.reshape(2, cap),
        frames.transpose(1, 0, 2), w_edge, b_edge.reshape(1, -1), w_message, w_update, w_readout,
        w_heads.T,
    )


def solution(mesh):
    placed = (
        P("dom", None),
        P(None, "dom"),
        P("dom", None),
        P("dom"),
        P("dom", None, None),
        P("frame", None, None),
        P(),
        P(),
        P(),
        P(),
        P(),
        P(),
    )
    body = functools.partial(local, mesh.shape["frame"], mesh.shape["dom"])
    return jax.shard_map(
        body, mesh=mesh, in_specs=placed, out_specs=P(None, "dom"), check_vma=False
    )
```
